128 devices in a mesh: batch: 16 (over z_lo, x, core), space: 8 (over y, z_hi).
Axes of the slice: x: 4, y: 4, z: 4 (z_hi: 2, z_lo: 2; z = z_hi * 2 + z_lo), core: 2. Of those that a mesh axis runs over, the one named last changes fastest.
Arguments:
- images: bfloat16 [16, 64, 256, 1024], P('batch', 'space'), may hold values from -6 to 6
- heights: int32 [16], P('batch'), may hold values from 32 to 64, as said below
- widths: int32 [16], P('batch'), may hold values from 512 to 1024, as said below
- conv_reduce: bfloat16 [2, 256, 64], replicated, may hold values from -0.375 to 0.375
- conv_spatial: bfloat16 [2, 3, 3, 64, 64], replicated, may hold values from -0.25 to 0.25
- conv_expand: bfloat16 [2, 64, 256], replicated, may hold values from -0.75 to 0.75
- scale_mid: float32 [2, 2, 64], replicated, may hold values from 0.25 to 1.75
- shift_mid: float32 [2, 2, 64], replicated, may hold values from -3 to 3
- scale_out: float32 [2, 256], replicated, may hold values from 0.25 to 1.75
- shift_out: float32 [2, 256], replicated, may hold values from -3 to 3
- cotangent: bfloat16 [16, 64, 256, 1024], P('batch', 'space'), may hold values from -6 to 6
Outputs:
- grad_images: bfloat16 [16, 64, 256, 1024], P('batch', 'space')
- grad_reduce: float32 [2, 256, 64], replicated
- grad_spatial: float32 [2, 3, 3, 64, 64], replicated
- grad_expand: float32 [2, 64, 256], replicated
The draws below stay inside these ranges and needn't reach their ends.
Inputs may be any that keep to these rules, and one draw needn't show every extreme that they name: `heights`: some image fills all 64 rows. `widths`: some image fills all 1024 columns.
All inputs are finite; a program needn't handle non-finite values.
Results may differ from the reference program's by a relative error of at most 0.015.
Values may be sent and summed in bfloat16 or wider, within the bound.
No kernel may reach another device: no remote copies, remote signals or barrier semaphores. Data moves between devices by JAX's collectives and lax.ppermute only.
A program may use at most 128 MiB of HBM per device.

```python
import math
import jax
import jax.numpy as jnp
from jax import lax

CH = 256
MID = 64
BLOCKS = 2
WIDTH = 1024
IMAGES = 16
HEIGHT = 64


def draw_heights(key, part):
    key = jax.random.fold_in(key, 11)
    first_key, second_key = jax.random.split(key)
    values = jax.random.randint(first_key, (IMAGES,), HEIGHT // 2, HEIGHT + 1)
    chosen = jax.random.randint(second_key, (), 0, IMAGES)
    return jnp.where(jnp.arange(IMAGES) == chosen, HEIGHT, values).astype(jnp.int32)


def draw_widths(key, part):
    key = jax.random.fold_in(key, 23)
    first_key, second_key = jax.random.split(key)
    values = jax.random.randint(first_key, (IMAGES,), WIDTH // 2, WIDTH + 1)
    chosen = jax.random.randint(second_key, (), 0, IMAGES)
    return jnp.where(jnp.arange(IMAGES) == chosen, WIDTH, values).astype(jnp.int32)


def levels(rng, dims, shards, least, largest):
    gain, own = 1.0, jax.random.fold_in(rng, 6)
    for position, shards_of in shards:
        steps = jnp.exp(jax.random.uniform(jax.random.fold_in(own, position), (shards_of,), jnp.float32, least / len(shards), largest / len(shards)))
        gain = gain * jnp.repeat(steps, dims[position] // shards_of).reshape([-1 if axis == position else 1 for axis in range(len(dims))])
    return gain


def normal_values(stream_key, dims, deviation, bound, cuts=(), held_as=jnp.bfloat16):
    result = deviation * jax.random.normal(stream_key, dims, jnp.float32)
    if cuts:
        result = result * levels(stream_key, dims, cuts, -0.22, 0.18)
    return jnp.clip(result, -bound, bound).astype(held_as)


def setup_inputs(seed: int = 0) -> dict:
    arg_keys = jax.random.split(jax.random.key(seed), 12)
    return {
        "images": normal_values(arg_keys[0], (IMAGES, HEIGHT, CH, WIDTH), 1.0, 6.0, ((0, 16), (1, 8))),
        "heights": draw_heights(jax.random.fold_in(arg_keys[11], 71), 0),
        "widths": draw_widths(jax.random.fold_in(arg_keys[11], 71), 0),
        "conv_reduce": normal_values(arg_keys[3], (BLOCKS, CH, MID), CH ** -0.5, 0.375),
        "conv_spatial": normal_values(arg_keys[4], (BLOCKS, 3, 3, MID, MID), (9 * MID) ** -0.5, 0.25),
        "conv_expand": normal_values(arg_keys[5], (BLOCKS, MID, CH), MID ** -0.5, 0.75),
        "scale_mid": jnp.clip(1.0 + 0.15 * jax.random.normal(arg_keys[6], (BLOCKS, 2, MID), jnp.float32), 0.25, 1.75),
        "shift_mid": normal_values(arg_keys[7], (BLOCKS, 2, MID), 0.5, 3.0, (), jnp.float32),
        "scale_out": jnp.clip(1.0 + 0.15 * jax.random.normal(arg_keys[8], (BLOCKS, CH), jnp.float32), 0.25, 1.75),
        "shift_out": normal_values(arg_keys[9], (BLOCKS, CH), 0.5, 3.0, (), jnp.float32),
        "cotangent": normal_values(arg_keys[10], (IMAGES, HEIGHT, CH, WIDTH), 1.0, 6.0, ((0, 16), (1, 8))),
    }


def silu_slope(value):
    sig = jax.nn.sigmoid(value)
    return sig + value * sig * (1.0 - sig)

def spatial_conv(padded, kernel, rows, cols):
    parts = [jnp.einsum('rcw,co->row', padded[row_shift:row_shift + rows, :, col_shift:col_shift + cols], kernel[row_shift, col_shift]) for row_shift in range(3) for col_shift in range(3)]
    return sum(parts)

def spatial_grad(padded, upstream, rows, cols):
    parts = [jnp.einsum('rcw,row->co', padded[row_shift:row_shift + rows, :, col_shift:col_shift + cols], upstream) for row_shift in range(3) for col_shift in range(3)]
    return jnp.stack(parts).reshape((3, 3) + parts[0].shape)

def spatial_back(padded_grad, kernel, rows, cols):
    parts = [jnp.einsum('row,co->rcw', padded_grad[2 - row_shift:2 - row_shift + rows, :, 2 - col_shift:2 - col_shift + cols], kernel[row_shift, col_shift]) for row_shift in range(3) for col_shift in range(3)]
    return sum(parts)

def image_pass(image, cot, height, width, conv_reduce, conv_spatial, conv_expand, scale_mid, shift_mid, scale_out, shift_out):
    f32 = jnp.float32
    bf16 = jnp.bfloat16
    row_ids = jnp.arange(HEIGHT, dtype=jnp.int32)
    col_ids = jnp.arange(WIDTH, dtype=jnp.int32)
    inside = ((row_ids < height)[:, None, None] & (col_ids < width)[None, None, :]).astype(f32)
    current = image
    saved = []
    for block_idx in range(BLOCKS):
        w_reduce = conv_reduce[block_idx].astype(f32)
        w_spatial = conv_spatial[block_idx].astype(f32)
        w_expand = conv_expand[block_idx].astype(f32)
        reduced = jnp.einsum('rcw,cm->rmw', current.astype(f32), w_reduce)
        pre_first = reduced * scale_mid[block_idx, 0][:, None] + shift_mid[block_idx, 0][:, None]
        first = (jax.nn.silu(pre_first) * inside).astype(bf16)
        padded = jnp.pad(first.astype(f32), ((1, 1), (0, 0), (1, 1)))
        spat = spatial_conv(padded, w_spatial, HEIGHT, WIDTH)
        pre_second = spat * scale_mid[block_idx, 1][:, None] + shift_mid[block_idx, 1][:, None]
        second = (jax.nn.silu(pre_second) * inside).astype(bf16)
        expanded = jnp.einsum('rmw,mc->rcw', second.astype(f32), w_expand)
        pre_out = expanded * scale_out[block_idx][:, None] + shift_out[block_idx][:, None] + current.astype(f32)
        output = (jax.nn.silu(pre_out) * inside).astype(bf16)
        saved.append((current, first, padded, second, pre_first, pre_second, pre_out))
        current = output
    upstream = cot
    g_reduce, g_spatial, g_expand = ([], [], [])
    for block_idx in reversed(range(BLOCKS)):
        block_in, first, padded, second, pre_first, pre_second, pre_out = saved[block_idx]
        w_reduce = conv_reduce[block_idx].astype(f32)
        w_spatial = conv_spatial[block_idx].astype(f32)
        w_expand = conv_expand[block_idx].astype(f32)
        grad_sum = upstream.astype(f32) * silu_slope(pre_out) * inside
        grad_exp = (grad_sum * scale_out[block_idx][:, None]).astype(bf16)
        g_expand.append(jnp.einsum('rmw,rcw->mc', second.astype(f32), grad_exp.astype(f32)))
        grad_second = jnp.einsum('rcw,mc->rmw', grad_exp.astype(f32), w_expand)
        grad_mid2 = (grad_second * silu_slope(pre_second) * inside * scale_mid[block_idx, 1][:, None]).astype(bf16)
        g_spatial.append(spatial_grad(padded, grad_mid2.astype(f32), HEIGHT, WIDTH))
        grad_padded = jnp.pad(grad_mid2.astype(f32), ((1, 1), (0, 0), (1, 1)))
        grad_first = spatial_back(grad_padded, w_spatial, HEIGHT, WIDTH)
        grad_mid1 = (grad_first * silu_slope(pre_first) * inside * scale_mid[block_idx, 0][:, None]).astype(bf16)
        g_reduce.append(jnp.einsum('rcw,rmw->cm', block_in.astype(f32), grad_mid1.astype(f32)))
        upstream = (grad_sum + jnp.einsum('rmw,cm->rcw', grad_mid1.astype(f32), w_reduce)).astype(bf16)
    grads = (jnp.stack(g_reduce[::-1]), jnp.stack(g_spatial[::-1]), jnp.stack(g_expand[::-1]))
    return (upstream, grads)

def reference(images, heights, widths, conv_reduce, conv_spatial, conv_expand, scale_mid, shift_mid, scale_out, shift_out, cotangent):

    def advance(carry, item):
        image, cot, height, width = item
        grad_image, grads = image_pass(image, cot, height, width, conv_reduce, conv_spatial, conv_expand, scale_mid, shift_mid, scale_out, shift_out)
        return (tuple((held + fresh for held, fresh in zip(carry, grads))), grad_image)
    start = (jnp.zeros((BLOCKS, CH, MID), jnp.float32), jnp.zeros((BLOCKS, 3, 3, MID, MID), jnp.float32), jnp.zeros((BLOCKS, MID, CH), jnp.float32))
    sums, grad_images = lax.scan(advance, start, (images, cotangent, heights, widths))
    factor = 1.0 / math.sqrt(IMAGES * HEIGHT * WIDTH)
    return (grad_images, sums[0] * factor, sums[1] * factor, sums[2] * factor)
```

```python
import math

import jax
import jax.numpy as jnp
from jax import lax
from jax.experimental import pallas as pl
from jax.experimental.pallas import tpu as pltpu
from jax.sharding import PartitionSpec as P

F32 = jnp.float32
BF16 = jnp.bfloat16
VMEM_LIMIT = 56 * 1024 * 1024
CHUNK = 256


def mm(a, b):
    return lax.dot_general(a, b, (((1,), (0,)), ((), ())), preferred_element_type=F32)


def mm_nt(a, b):
    return lax.dot_general(a, b, (((1,), (1,)), ((), ())), preferred_element_type=F32)


def gate(h):
    t = jnp.tanh(h)
    p = 1 + t
    y = h * p
    return y, p + y * (1 - t)


def row_mask(heights, widths, row, rows, cols):
    where = lax.axis_index("space") * rows + row
    limit = jnp.where(where < heights[0], widths[0], 0)
    ids = lax.broadcasted_iota(jnp.int32, (1, cols), 1)
    return jnp.where(ids < limit, 1.0, 0.0).astype(BF16)


def shifted(v):
    cols = v.shape[-1]
    ids = lax.broadcasted_iota(jnp.int32, (1, cols), 1)
    not_first = jnp.where(ids > 0, 1.0, 0.0).astype(BF16)
    not_last = jnp.where(ids < cols - 1, 1.0, 0.0).astype(BF16)
    return pltpu.roll(v, 1, 1) * not_first, pltpu.roll(v, cols - 1, 1) * not_last


def edge_flags():
    me = lax.axis_index("space")
    top = jnp.where(me > 0, 1.0, 0.0).astype(BF16)
    bottom = jnp.where(me < lax.axis_size("space") - 1, 1.0, 0.0).astype(BF16)
    return top, bottom


def fill_padded(pad, strip, above, below, rows):
    top, bottom = edge_flags()
    pad[0] = above[...] * top
    for r in range(rows):
        pad[r + 1] = strip[r]
    pad[rows + 1] = below[...] * bottom


def stack_shifts(out, pad, flip):
    for r in range(out.shape[0]):
        v = pad[r]
        mid = v.shape[0]
        before, after = shifted(v)
        out[r, :mid] = after if flip else before
        out[r, mid : 2 * mid] = v
        out[r, 2 * mid :] = before if flip else after


def chunks(cols):
    return [slice(c, c + CHUNK) for c in range(0, cols, CHUNK)]


def taps(stacked, row, cut):
    part = stacked[pl.ds(row, 3), :, cut]
    return part.reshape(part.shape[0] * part.shape[1], part.shape[2])


def reduce_row(x, w_reduce, b_first, mask, first, slope, cut):
    h = (mm(w_reduce[...], x) + b_first[...]).astype(BF16)
    y, d = gate(h)
    first[:, cut] = y * mask[:, cut]
    slope[:, cut] = d * mask[:, cut]


def k1(rows, row_of, n_alias, heights, widths, x, w_reduce, b_first, *rest):
    (first, slope), edges, _ = parts_of(rest, n_alias, 2)
    step = pl.program_id(0)
    cols = x.shape[-1]
    mask = row_mask(heights, widths, row_of(step), rows, cols)
    for cut in chunks(cols):
        reduce_row(x[0, :, cut], w_reduce, b_first, mask, first.at[0], slope.at[0], cut)
    emit_edges(step, first, edges)


def parts_of(rest, n_alias, n_out):
    refs = rest[n_alias:]
    n_edge = 0 if n_alias else 2
    return refs[:n_out], refs[n_out : n_out + n_edge], refs[n_out + n_edge :]


def emit_edges(step, value, edges):
    if not edges:
        return
    top, bottom = edges

    @pl.when(step == 0)
    def _():
        top[...] = value[0]

    @pl.when(step == 1)
    def _():
        bottom[...] = value[0]


def k2(rows, row_of, n_alias, heights, widths, first0, above, below, x, kf, b_second, we, b_out,
       w_reduce, b_first, *rest):
    (second, slope2, slope3, x1, first1, slope1), edges, (pad, stack) = parts_of(rest, n_alias, 6)
    step = pl.program_id(0)
    row = row_of(step)
    cols = x.shape[-1]

    @pl.when(step == 0)
    def _():
        fill_padded(pad, first0, above, below, rows)
        stack_shifts(stack, pad, False)

    mask = row_mask(heights, widths, row, rows, cols)
    for cut in chunks(cols):
        h = (mm(kf[...], taps(stack, row, cut)) + b_second[...]).astype(BF16)
        y, d = gate(h)
        second[0, :, cut] = y
        slope2[0, :, cut] = d
        h = (mm(we[...], y) + b_out[...]).astype(BF16) + x[0, :, cut] * 0.5
        y, d = gate(h)
        slope3[0, :, cut] = d
        x1[0, :, cut] = y
        reduce_row(y, w_reduce, b_first, mask, first1.at[0], slope1.at[0], cut)
    emit_edges(step, first1, edges)


def k3(rows, row_of, n_alias, heights, widths, first1, above, below, x1, cot, kf, b_second, we,
       b_out, we_back, *rest):
    (gsum, gmid2, dexp), edges, (pad, stack) = parts_of(rest, n_alias, 3)
    step = pl.program_id(0)
    row = row_of(step)
    cols = x1.shape[-1]

    @pl.when(step == 0)
    def _():
        fill_padded(pad, first1, above, below, rows)
        stack_shifts(stack, pad, False)
        if n_alias:
            dexp[...] = rest[n_alias - 1][...]
        else:
            dexp[...] = jnp.zeros_like(dexp)

    mask = row_mask(heights, widths, row, rows, cols)
    for cut in chunks(cols):
        h = (mm(kf[...], taps(stack, row, cut)) + b_second[...]).astype(BF16)
        y2, d2 = gate(h)
        h = (mm(we[...], y2) + b_out[...]).astype(BF16) + x1[0, :, cut] * 0.5
        _, d3 = gate(h)
        g = cot[0, :, cut] * mask[:, cut] * d3
        gsum[0, :, cut] = g
        gmid2[0, :, cut] = mm(we_back[...], g).astype(BF16) * d2
        dexp[...] += mm_nt(y2, g)
    emit_edges(step, gmid2, edges)


def k4(rows, row_of, n_alias, heights, widths, gmid2, above, below, first1, f_above, f_below,
       slope1, x1, gsum1, slope3, slope2, second, kb, wr_back, we_back, *rest):
    (gsum0, gmid20, dred, dspat, dexp), edges, (pad, stack, fpad) = parts_of(rest, n_alias, 5)
    step = pl.program_id(0)
    row = row_of(step)
    cols = x1.shape[-1]

    @pl.when(step == 0)
    def _():
        fill_padded(pad, gmid2, above, below, rows)
        stack_shifts(stack, pad, True)
        fill_padded(fpad, first1, f_above, f_below, rows)
        if n_alias:
            dred[...] = rest[n_alias - 3][...]
            dspat[...] = rest[n_alias - 2][...]
            dexp[...] = rest[n_alias - 1][...]
        else:
            dred[...] = jnp.zeros_like(dred)
            dspat[...] = jnp.zeros_like(dspat)
            dexp[...] = jnp.zeros_like(dexp)

    mask = row_mask(heights, widths, row, rows, cols)
    for cut in chunks(cols):
        g1 = mm(kb[...], taps(stack, row, cut)).astype(BF16) * slope1[0, :, cut]
        dred[...] += mm_nt(g1, x1[0, :, cut])
        up = (mm(wr_back[...], g1) + gsum1[0, :, cut].astype(F32)).astype(BF16)
        g = up * slope3[0, :, cut] * mask[:, cut]
        gsum0[0, :, cut] = g
        gmid20[0, :, cut] = mm(we_back[...], g).astype(BF16) * slope2[0, :, cut]
        dexp[...] += mm_nt(second[0, :, cut], g)
        dspat[...] += mm_nt(taps(fpad, row, cut), stack[row + 1, :, cut])
    emit_edges(step, gmid20, edges)


def k5(rows, gmid2, above, below, first0, f_above, f_below, slope1, x, kb, gmid1, dred, dspat,
       pad, stack, fpad):
    row = pl.program_id(0)
    cols = x.shape[-1]

    @pl.when(row == 0)
    def _():
        fill_padded(pad, gmid2, above, below, rows)
        stack_shifts(stack, pad, True)
        fill_padded(fpad, first0, f_above, f_below, rows)
        dred[...] = jnp.zeros_like(dred)
        dspat[...] = jnp.zeros_like(dspat)

    for cut in chunks(cols):
        g1 = mm(kb[...], taps(stack, row, cut)).astype(BF16) * slope1[0, :, cut]
        gmid1[0, :, cut] = g1
        dred[...] += mm_nt(g1, x[0, :, cut])
        dspat[...] += mm_nt(taps(fpad, row, cut), stack[row + 1, :, cut])


def k6(gmid1, gsum, wr_back, out):
    cols = gmid1.shape[-1]
    for cut in chunks(cols):
        acc = mm(wr_back[...], gmid1[0, :, cut]) + gsum[0, :, cut].astype(F32) * 0.25
        out[0, :, cut] = acc.astype(BF16)


def whole(a):
    return pl.BlockSpec(a.shape, lambda i, n=a.ndim: (0,) * n)


def by_row(a, row_of):
    return pl.BlockSpec((1,) + a.shape[1:], lambda i, n=a.ndim: (row_of(i),) + (0,) * (n - 1))


SMEM = pl.BlockSpec(memory_space=pltpu.SMEM)
ANY = pl.BlockSpec(memory_space=pl.ANY)


def strip_call(kernel, steps, row_of, args, outs, scratch, carried, name):
    specs = {"row": lambda a: by_row(a, row_of), "whole": whole, "smem": lambda a: SMEM}
    out_shapes = [jax.ShapeDtypeStruct(s, d) for s, d, _ in outs]
    aliases = {}
    extra, extra_specs = [], []
    if carried is not None:
        for idx, (value, (_, _, kind)) in enumerate(zip(carried, outs)):
            aliases[len(args) + idx] = idx
            extra.append(value)
            extra_specs.append(ANY if kind == "row" else whole(value))
    return pl.pallas_call(
        kernel,
        grid=(steps,),
        in_specs=[specs[k](a) for a, k in args] + extra_specs,
        out_specs=[specs[k](s) for s, (_, _, k) in zip(out_shapes, outs)],
        out_shape=out_shapes,
        scratch_shapes=scratch,
        input_output_aliases=aliases,
        compiler_params=pltpu.CompilerParams(vmem_limit_bytes=VMEM_LIMIT),
        name=name,
    )(*[a for a, _ in args], *extra)


def split_call(make, rows, args, outs, edge_shape, scratch, name):
    edge_row = lambda i: i * (rows - 1)
    inner_row = lambda i: i + 1
    edges = [(edge_shape, BF16, "whole")] * 2
    early = strip_call(make(edge_row, 0), 2, edge_row, args, outs + edges, scratch, None, name + "_edge")
    top, bottom = early[-2:]
    count = lax.axis_size("space")
    above = lax.ppermute(bottom, "space", [(i, (i + 1) % count) for i in range(count)])
    below = lax.ppermute(top, "space", [((i + 1) % count, i) for i in range(count)])
    late = strip_call(make(inner_row, len(outs)), rows - 2, inner_row, args, outs, scratch, early[:-2], name + "_inner")
    return late, above, below


def all_sum(value):
    for axis, bit in (("batch", 1), ("batch", 2), ("space", 2), ("batch", 8), ("batch", 4), ("space", 4), ("space", 1)):
        n = lax.axis_size(axis)
        value = value + lax.ppermute(value.astype(BF16), axis, [(i, i ^ bit) for i in range(n)]).astype(F32)
    return value


def body(images, heights, widths, conv_reduce, conv_spatial, conv_expand, scale_mid, shift_mid,
         scale_out, shift_out, cotangent):
    _, rows, chans, cols = images.shape
    mid = conv_reduce.shape[-1]
    x0 = images[0]
    cot = cotangent[0]
    red, spa, exp = (a.astype(F32) for a in (conv_reduce, conv_spatial, conv_expand))
    wr, kf, we, we_back, kb, wr_back, b1, b2, b3 = ([] for _ in range(9))
    for k in range(2):
        twice = 2.0 ** (2 - k)
        s1, s2, so = scale_mid[k, 0], scale_mid[k, 1], scale_out[k]
        wr.append((red[k] * (0.5 * s1)).T.astype(BF16))
        kf.append((spa[k] * (0.5 * s2)).transpose(3, 0, 1, 2).reshape(mid, -1).astype(BF16))
        we.append((exp[k] * (0.5 * so)).T.astype(BF16))
        we_back.append((exp[k] * so * s2[:, None] * (0.5 / twice)).astype(BF16))
        kb.append((spa[k, ::-1] * (0.5 * s1)[:, None]).transpose(2, 0, 1, 3).reshape(mid, -1).astype(BF16))
        wr_back.append((red[k] * (1.0 if k == 0 else twice)).astype(BF16))
        b1.append(0.5 * shift_mid[k, 0][:, None])
        b2.append(0.5 * shift_mid[k, 1][:, None])
        b3.append(0.5 * shift_out[k][:, None])
    small = (rows, mid, cols)
    large = (rows, chans, cols)
    edge = (mid, cols)
    hw = [(heights, "smem"), (widths, "smem")]
    pad = pltpu.VMEM((rows + 2, mid, cols), BF16)
    stack = pltpu.VMEM((rows + 2, 3 * mid, cols), BF16)
    acc_c = ((mid, chans), F32, "whole")
    acc_s = ((3 * mid, 3 * mid), F32, "whole")

    def bind(kernel):
        import functools
        return lambda row_of, n: functools.partial(kernel, rows, row_of, n)

    (first0, slope1_0), f0a, f0b = split_call(
        bind(k1), rows, hw + [(x0, "row"), (wr[0], "whole"), (b1[0], "whole")],
        [(small, BF16, "row"), (small, BF16, "row")], edge, [], "reduce")
    (second0, slope2_0, slope3_0, x1, first1, slope1_1), f1a, f1b = split_call(
        bind(k2), rows,
        hw + [(first0, "whole"), (f0a, "whole"), (f0b, "whole"), (x0, "row"), (kf[0], "whole"), (b2[0], "whole"),
              (we[0], "whole"), (b3[0], "whole"), (wr[1], "whole"), (b1[1], "whole")],
        [(small, BF16, "row"), (small, BF16, "row"), (large, BF16, "row"), (large, BF16, "row"), (small, BF16, "row"), (small, BF16, "row")],
        edge, [pad, stack], "forward")
    (gsum1, gmid2_1, dexp1), g1a, g1b = split_call(
        bind(k3), rows,
        hw + [(first1, "whole"), (f1a, "whole"), (f1b, "whole"), (x1, "row"), (cot, "row"), (kf[1], "whole"), (b2[1], "whole"),
              (we[1], "whole"), (b3[1], "whole"), (we_back[1], "whole")],
        [(large, BF16, "row"), (small, BF16, "row"), acc_c], edge, [pad, stack], "turn")
    (gsum0, gmid2_0, dred1, dspat1, dexp0), g0a, g0b = split_call(
        bind(k4), rows,
        hw + [(gmid2_1, "whole"), (g1a, "whole"), (g1b, "whole"), (first1, "whole"), (f1a, "whole"), (f1b, "whole"),
              (slope1_1, "row"), (x1, "row"), (gsum1, "row"), (slope3_0, "row"), (slope2_0, "row"), (second0, "row"),
              (kb[1], "whole"), (wr_back[1], "whole"), (we_back[0], "whole")],
        [(large, BF16, "row"), (small, BF16, "row"), acc_c, acc_s, acc_c], edge, [pad, stack, pad], "backward")
    import functools
    same = lambda i: i
    gmid1_0, dred0, dspat0 = strip_call(
        functools.partial(k5, rows), rows, same,
        [(gmid2_0, "whole"), (g0a, "whole"), (g0b, "whole"), (first0, "whole"), (f0a, "whole"), (f0b, "whole"),
         (slope1_0, "row"), (x0, "row"), (kb[0], "whole")],
        [(small, BF16, "row"), acc_c, acc_s], [pad, stack, pad], None, "last")
    (grad,) = strip_call(
        k6, rows, same, [(gmid1_0, "row"), (gsum0, "row"), (wr_back[0], "whole")],
        [(large, BF16, "row")], [], None, "grad_images")
    terms = jnp.concatenate(
        [dred0, dred1, dexp0, dexp1] + [jnp.pad(d, ((0, 0), (0, chans - 3 * mid))) for d in (dspat0, dspat1)])
    summed = all_sum(terms)
    factor = 1.0 / math.sqrt(lax.axis_size("batch") * rows * lax.axis_size("space") * cols)
    summed = summed * factor
    g_reduce = jnp.stack([summed[:mid].T, summed[mid : 2 * mid].T])
    g_expand = jnp.stack([summed[2 * mid : 3 * mid] * (scale_out[0] * 0.25), summed[3 * mid : 4 * mid] * (scale_out[1] * 0.5)])
    g_spatial = summed[4 * mid :, : 3 * mid].reshape(2, 3, mid, 3, mid).transpose(0, 1, 3, 2, 4)
    return grad[None], g_reduce, g_spatial, g_expand


def solution(mesh):
    strips = P("batch", "space", None, None)
    placed = (strips, P("batch"), P("batch")) + (P(),) * 7 + (strips,)
    return jax.shard_map(
        body, mesh=mesh, in_specs=placed, out_specs=(strips, P(), P(), P()), check_vma=False)
```

```python
import functools
import math

import jax
import jax.numpy as jnp
from jax import lax
from jax.experimental import pallas as pl
from jax.experimental.pallas import tpu as pltpu
from jax.sharding import PartitionSpec as P

F32 = jnp.float32
BF16 = jnp.bfloat16
VMEM_LIMIT = 12 * 1024 * 1024
CHUNK = 256
VMEM = pl.BlockSpec(memory_space=pltpu.VMEM)
SMEM = pl.BlockSpec(memory_space=pltpu.SMEM)
HBM = pl.BlockSpec(memory_space=pltpu.HBM)


def mm(a, b):
    return lax.dot_general(a, b, (((1,), (0,)), ((), ())), preferred_element_type=F32)


def mm_nt(a, b):
    return lax.dot_general(a, b, (((1,), (1,)), ((), ())), preferred_element_type=F32)


def gate(h):
    t = jnp.tanh(h)
    p = 1 + t
    y = h * p
    return y, p + y * (1 - t)


def wide(bias, cols):
    return jnp.concatenate([bias[...]] * (cols // bias.shape[-1]), axis=1)


def row_mask(heights, widths, row, rows, cols):
    where = lax.axis_index("space") * rows + row
    limit = jnp.where(where < heights[0], widths[0], 0)
    ids = lax.broadcasted_iota(jnp.int32, (1, cols), 1)
    return jnp.where(ids < limit, 1.0, 0.0).astype(BF16)


def before(v):
    ids = lax.broadcasted_iota(jnp.int32, (1, v.shape[-1]), 1)
    return pltpu.roll(v, 1, 1) * jnp.where(ids > 0, 1.0, 0.0).astype(v.dtype)


def after(v):
    cols = v.shape[-1]
    ids = lax.broadcasted_iota(jnp.int32, (1, cols), 1)
    return pltpu.roll(v, cols - 1, 1) * jnp.where(ids < cols - 1, 1.0, 0.0).astype(v.dtype)


def edge_taps(strip, halo_above, halo_below, last):
    me = lax.axis_index("space")
    rows = strip.shape[0]
    if last:
        have = jnp.where(me < lax.axis_size("space") - 1, 1.0, 0.0).astype(BF16)
        parts = [strip[rows - 2], strip[rows - 1], halo_below[...] * have]
    else:
        have = jnp.where(me > 0, 1.0, 0.0).astype(BF16)
        parts = [halo_above[...] * have, strip[0], strip[1]]
    return jnp.concatenate(parts, axis=0)


def inner_taps(strip, row, count):
    part = strip[pl.ds(row - 1, count)]
    return part.reshape(part.shape[0] * part.shape[1], part.shape[2])


def join(out, flip):
    mid = out.shape[0] // 3
    first, centre, last = out[:mid], out[mid : 2 * mid], out[2 * mid :]
    if flip:
        first, last = last, first
    return before(first) + centre + after(last)


def spread(v):
    return jnp.concatenate([after(v), v, before(v)], axis=0)


def chunks(cols):
    return [slice(c, c + CHUNK) for c in range(0, cols, CHUNK)]


def reduce_part(x, w_reduce, b_first, mask):
    h = (mm(w_reduce[...], x) + wide(b_first, CHUNK)).astype(BF16)
    y, d = gate(h)
    return y * mask, d * mask


def conv_rows(edges, rows, strip, halos, single, double, flip, work):
    if edges:
        for last in (False, True):
            taps = edge_taps(strip, *halos, last)
            work(rows - 1 if last else 0, int(last), join(mm(single[...], taps), flip))
        return

    def pair(i, carry):
        row = 1 + 2 * i
        out = mm(double[...], inner_taps(strip, row, 4))
        half = out.shape[0] // 2
        work(row, row - 1, join(out[:half], flip))
        work(row + 1, row, join(out[half:], flip))
        return carry

    lax.fori_loop(0, (rows - 2) // 2, pair, 0)


def taps_of(edges, strip, halos, row):
    return edge_taps(strip, *halos, row > 0) if edges else inner_taps(strip, row, 3)


def start_sums(have, sums):
    for value, out in zip(have or [None] * len(sums), sums):
        out[...] = jnp.zeros_like(out) if value is None else value[...]


def gather_rows(full, inner, top, bottom):
    rows = full.shape[0]
    full[0] = top[...]
    full[rows - 1] = bottom[...]
    for r in range(1, rows - 1):
        full[r] = inner[r - 1]


def forward_rows(edges, hw, strip, halos, x, kf, kf2, b_second, we, b_out, w_reduce, b_first,
                 second, slope2, slope3, x1, slope1, put_first):
    rows, cols = x.shape[0], x.shape[-1]

    def work(row, slot, pre):
        mask = row_mask(*hw, row, rows, cols)
        for cut in chunks(cols):
            h = (pre[:, cut] + wide(b_second, CHUNK)).astype(BF16)
            y, d = gate(h)
            second[slot, :, cut] = y
            slope2[slot, :, cut] = d
            h = (mm(we[...], y) + wide(b_out, CHUNK)).astype(BF16) + x[row, :, cut] * 0.5
            y, d = gate(h)
            slope3[slot, :, cut] = d
            x1[slot, :, cut] = y
            first, slope1[slot, :, cut] = reduce_part(y, w_reduce, b_first, mask[:, cut])
            put_first(row, slot, cut, first)

    conv_rows(edges, rows, strip, halos, kf, kf2, False, work)


def forward_inner(heights, widths, x, top, bottom, kf, kf2, b2, we, b3, wr, b1,
                  first0, slope1_0, second, slope2, slope3, x1, slope1_1, first1):
    rows, cols = x.shape[0], x.shape[-1]
    first0[0] = top[...]
    first0[rows - 1] = bottom[...]

    @pl.loop(1, rows - 1)
    def _(row):
        mask = row_mask(heights, widths, row, rows, cols)
        for cut in chunks(cols):
            first0[row, :, cut], slope1_0[row - 1, :, cut] = reduce_part(
                x[row, :, cut], wr.at[0], b1.at[0], mask[:, cut])

    def put_first(row, slot, cut, value):
        first1[slot, :, cut] = value

    forward_rows(False, (heights, widths), first0, None, x, kf.at[0], kf2.at[0], b2.at[0], we.at[0], b3.at[0],
                 wr.at[1], b1.at[1], second, slope2, slope3, x1, slope1_1, put_first)


def forward_edge(heights, widths, x, first0, above, below, first1_inner, kf, kf2, b2, we, b3, wr, b1,
                 second, slope2, slope3, x1, slope1_1, first1, top, bottom):
    def put_first(row, slot, cut, value):
        (bottom if slot else top)[:, cut] = value

    forward_rows(True, (heights, widths), first0, (above, below), x, kf.at[0], kf2.at[0], b2.at[0], we.at[0],
                 b3.at[0], wr.at[1], b1.at[1], second, slope2, slope3, x1, slope1_1, put_first)
    gather_rows(first1, first1_inner, top, bottom)


def turn_rows(edges, hw, first1, halos, x1, cot, kf, kf2, b2, we, b3, we_back, gsum, dexp, put_mid2):
    rows, cols = cot.shape[0], cot.shape[-1]

    def work(row, slot, pre):
        mask = row_mask(*hw, row, rows, cols)
        for cut in chunks(cols):
            h = (pre[:, cut] + wide(b2.at[1], CHUNK)).astype(BF16)
            y2, d2 = gate(h)
            h = (mm(we[1], y2) + wide(b3.at[1], CHUNK)).astype(BF16) + x1[slot, :, cut] * 0.5
            _, d3 = gate(h)
            g = cot[row, :, cut] * mask[:, cut] * d3
            gsum[slot, :, cut] = g
            put_mid2(row, slot, cut, mm(we_back[1], g).astype(BF16) * d2)
            dexp[...] += mm_nt(y2, g)

    conv_rows(edges, rows, first1, halos, kf.at[1], kf2.at[1], False, work)


def turn_inner(heights, widths, first1, x1, cot, kf, kf2, b2, we, b3, we_back, gsum, gmid2, dexp):
    start_sums(None, [dexp])

    def put_mid2(row, slot, cut, value):
        gmid2[slot, :, cut] = value

    turn_rows(False, (heights, widths), first1, None, x1, cot, kf, kf2, b2, we, b3, we_back, gsum, dexp, put_mid2)


def turn_edge(heights, widths, first1, above, below, x1, cot, kf, kf2, b2, we, b3, we_back, gmid2_inner, dexp_inner,
              gsum, gmid2, dexp, top, bottom):
    start_sums([dexp_inner], [dexp])

    def put_mid2(row, slot, cut, value):
        (bottom if slot else top)[:, cut] = value

    turn_rows(True, (heights, widths), first1, (above, below), x1, cot, kf, kf2, b2, we, b3, we_back, gsum, dexp, put_mid2)
    gather_rows(gmid2, gmid2_inner, top, bottom)


def backward_rows(edges, hw, gmid2, g_halos, first1, f_halos, slope1, x1, gsum1, slope3, slope2, second,
                  kb, kb2, wr_back, we_back, gsum0, dred, dspat, dexp, put_mid2):
    rows, cols = gmid2.shape[0], gmid2.shape[-1]

    def work(row, slot, back):
        mask = row_mask(*hw, row, rows, cols)
        for cut in chunks(cols):
            g1 = back[:, cut].astype(BF16) * slope1[slot, :, cut]
            dred[...] += mm_nt(g1, x1[slot, :, cut])
            up = (mm(wr_back[1], g1) + gsum1[slot, :, cut].astype(F32)).astype(BF16)
            g = up * slope3[slot, :, cut] * mask[:, cut]
            gsum0[slot, :, cut] = g
            put_mid2(row, slot, cut, mm(we_back[0], g).astype(BF16) * slope2[slot, :, cut])
            dexp[...] += mm_nt(second[slot, :, cut], g)
        dspat[...] += mm_nt(taps_of(edges, first1, f_halos, row), spread(gmid2[row]))

    conv_rows(edges, rows, gmid2, g_halos, kb.at[1], kb2.at[1], True, work)


def backward_inner(heights, widths, gmid2, first1, slope1, x1, gsum1, slope3, slope2, second, kb, kb2, wr_back, we_back,
                   gsum0, gmid2_0, dred, dspat, dexp):
    start_sums(None, [dred, dspat, dexp])

    def put_mid2(row, slot, cut, value):
        gmid2_0[slot, :, cut] = value

    backward_rows(False, (heights, widths), gmid2, None, first1, None, slope1, x1, gsum1, slope3, slope2, second,
                  kb, kb2, wr_back, we_back, gsum0, dred, dspat, dexp, put_mid2)


def backward_edge(heights, widths, gmid2, above, below, first1, f_above, f_below, slope1, x1, gsum1, slope3, slope2, second,
                  kb, kb2, wr_back, we_back, gmid2_inner, dred_inner, dspat_inner, dexp_inner,
                  gsum0, gmid2_0, dred, dspat, dexp, top, bottom):
    start_sums([dred_inner, dspat_inner, dexp_inner], [dred, dspat, dexp])

    def put_mid2(row, slot, cut, value):
        (bottom if slot else top)[:, cut] = value

    backward_rows(True, (heights, widths), gmid2, (above, below), first1, (f_above, f_below), slope1, x1, gsum1, slope3,
                  slope2, second, kb, kb2, wr_back, we_back, gsum0, dred, dspat, dexp, put_mid2)
    gather_rows(gmid2_0, gmid2_inner, top, bottom)


def last_rows(edges, gmid2, g_halos, first0, f_halos, slope1, x, kb, kb2, gmid1, dred, dspat):
    def work(row, slot, back):
        g1 = back.astype(BF16) * slope1[slot]
        gmid1[slot] = g1
        dred[...] += mm_nt(g1, x[row])
        dspat[...] += mm_nt(taps_of(edges, first0, f_halos, row), spread(gmid2[row]))

    conv_rows(edges, x.shape[0], gmid2, g_halos, kb.at[0], kb2.at[0], True, work)


def last_inner(gmid2, first0, slope1, x, kb, kb2, gmid1, dred, dspat):
    start_sums(None, [dred, dspat])
    last_rows(False, gmid2, None, first0, None, slope1, x, kb, kb2, gmid1, dred, dspat)


def last_edge(gmid2, above, below, first0, f_above, f_below, slope1, x, kb, kb2, dred_inner, dspat_inner,
              dred1, dexp0, dexp1, dspat1, gmid1, terms, dred, dspat):
    start_sums([dred_inner, dspat_inner], [dred, dspat])
    last_rows(True, gmid2, (above, below), first0, (f_above, f_below), slope1, x, kb, kb2, gmid1, dred, dspat)
    at = 0
    for value in (dred, dred1, dexp0, dexp1, dspat, dspat1):
        tall, across = value.shape
        terms[at : at + tall, :across] = value[...].astype(BF16)
        if across < terms.shape[1]:
            terms[at : at + tall, across:] = jnp.zeros((tall, terms.shape[1] - across), BF16)
        at += tall


def grad_rows(gmid1_inner, gmid1_edge, gsum_inner, gsum_edge, wr_back, out, held, sems):
    rows, cols = held.shape[0], held.shape[-1]

    def work(row, slot, gmid1, gsum):
        for cut in chunks(cols):
            acc = mm(wr_back[0], gmid1[slot, :, cut]) + gsum[slot, :, cut].astype(F32) * 0.25
            held[row, :, cut] = acc.astype(BF16)
        pltpu.make_async_copy(held.at[row], out.at[row], sems.at[row]).start()

    @pl.loop(1, rows - 1)
    def _(row):
        work(row, row - 1, gmid1_inner, gsum_inner)

    work(0, 0, gmid1_edge, gsum_edge)
    work(rows - 1, 1, gmid1_edge, gsum_edge)
    for r in range(rows):
        pltpu.make_async_copy(held.at[r], out.at[r], sems.at[r]).wait()


def finish(factor, terms, scale_out, g_reduce, g_spatial, g_expand):
    mid = g_reduce.shape[1]
    for k in range(2):
        g_reduce[k] = terms[k * mid : (k + 1) * mid].astype(F32) * factor
        scale = scale_out[k : k + 1, :] * (factor * 0.5 ** (2 - k))
        g_expand[k] = terms[(2 + k) * mid : (3 + k) * mid].astype(F32) * scale
        base = (4 + 3 * k) * mid
        for a in range(3):
            for b in range(3):
                part = terms[base + a * mid : base + (a + 1) * mid, b * mid : (b + 1) * mid]
                g_spatial[k, a, b] = part.astype(F32) * factor


def lanes(vector, count):
    return jnp.broadcast_to(vector, (count, vector.shape[-1])).T


def start(heights, widths, images, red_h, spa_h, exp_h, sm_h, sh_h, so_h, sho_h,
          wr, kf, kf2, we, we_back, kb, kb2, wr_back, b1, b2, b3, x, slope1, top, bottom,
          red, spa, exp, scale_mid, shift_mid, scale_out, shift_out, sems):
    rows, cols = x.shape[0], x.shape[-1]
    params = list(zip((red_h, spa_h, exp_h, sm_h, sh_h, so_h, sho_h),
                      (red, spa, exp, scale_mid, shift_mid, scale_out, shift_out)))
    small = [pltpu.make_async_copy(s, d, sems.at[rows + n]) for n, (s, d) in enumerate(params)]
    strips = [pltpu.make_async_copy(images.at[r], x.at[r], sems.at[r]) for r in range(rows)]
    for copy in small:
        copy.start()
    for r in (0, rows - 1, *range(1, rows - 1)):
        strips[r].start()
    for copy in small:
        copy.wait()
    mid = red.shape[1]
    kf2[...] = jnp.zeros_like(kf2)
    kb2[...] = jnp.zeros_like(kb2)
    for k in range(2):
        twice = 2.0 ** (2 - k)
        s1, s2 = scale_mid[k, 0:1, :], scale_mid[k, 1:2, :]
        so = scale_out[k : k + 1, :]
        r, e = red[k].astype(F32), exp[k].astype(F32)
        chans = r.shape[-1]
        wr[k] = (r * (0.5 * lanes(s1, chans))).astype(BF16)
        wr_back[k] = (r * (1.0 if k == 0 else twice)).T.astype(BF16)
        we[k] = (e * (0.5 * so)).T.astype(BF16)
        we_back[k] = (e * (so * (0.5 / twice)) * lanes(s2, chans)).astype(BF16)
        half = 0.5 * lanes(s1, mid)
        for a in range(3):
            for b in range(3):
                part = spa[k, a, b].astype(F32)
                ahead = (part * (0.5 * s2)).T.astype(BF16)
                back = (part * half).astype(BF16)
                for out, out2, value, at in ((kf, kf2, ahead, a), (kb, kb2, back, 2 - a)):
                    out[k, b * mid : (b + 1) * mid, at * mid : (at + 1) * mid] = value
                    for j in range(2):
                        out2[k, (3 * j + b) * mid : (3 * j + b + 1) * mid, (at + j) * mid : (at + j + 1) * mid] = value
        b1[k] = 0.5 * lanes(shift_mid[k, 0:1, :], b1.shape[-1])
        b2[k] = 0.5 * lanes(shift_mid[k, 1:2, :], b2.shape[-1])
        b3[k] = 0.5 * lanes(shift_out[k : k + 1, :], b3.shape[-1])
    for slot, (row, edge) in enumerate(((0, top), (rows - 1, bottom))):
        strips[row].wait()
        mask = row_mask(heights, widths, row, rows, cols)
        for cut in chunks(cols):
            edge[:, cut], slope1[slot, :, cut] = reduce_part(x[row, :, cut], wr.at[0], b1.at[0], mask[:, cut])
    for r in range(1, rows - 1):
        strips[r].wait()


def call(kernel, outs, args, name, specs=None, out_specs=None, scratch=(), limit=VMEM_LIMIT):
    return pl.pallas_call(
        kernel,
        in_specs=specs or [VMEM] * len(args),
        out_specs=out_specs or [VMEM] * len(outs),
        out_shape=[jax.ShapeDtypeStruct(s, d) for s, d in outs],
        scratch_shapes=list(scratch),
        compiler_params=pltpu.CompilerParams(vmem_limit_bytes=limit),
        name=name,
    )(*args)


def placed_call(kernel, outs, args, name):
    return call(kernel, outs, args, name, [SMEM] * 2 + [VMEM] * (len(args) - 2))


def exchange(top, bottom):
    count = lax.axis_size("space")
    above = lax.ppermute(bottom, "space", [(i, (i + 1) % count) for i in range(count)])
    below = lax.ppermute(top, "space", [((i + 1) % count, i) for i in range(count)])
    return above, below


def all_sum(terms):
    n = lax.axis_size("batch")
    tall, across = terms.shape
    shares = lax.all_to_all(terms.reshape(n, tall // n, across), "batch", 0, 0, tiled=True)
    share = shares.astype(F32).sum(0)
    count = lax.axis_size("space")
    for bit in (2, 6, 1):
        share = share + lax.ppermute(share.astype(BF16), "space", [(i, i ^ bit) for i in range(count)]).astype(F32)
    spread_out = jnp.broadcast_to(share.astype(BF16)[None], (n,) + share.shape)
    return lax.all_to_all(spread_out, "batch", 0, 0, tiled=True).reshape(terms.shape)


def body(images, heights, widths, conv_reduce, conv_spatial, conv_expand, scale_mid, shift_mid,
         scale_out, shift_out, cotangent):
    _, rows, chans, cols = images.shape
    mid = conv_reduce.shape[-1]
    cot = cotangent[0]
    wide_w, tall_w = ((mid, chans), BF16), ((chans, mid), BF16)
    single, double = ((3 * mid, 3 * mid), BF16), ((6 * mid, 4 * mid), BF16)
    bias = ((mid, 128), F32)
    made = [wide_w, single, double, tall_w, wide_w, single, double, tall_w, bias, bias, ((chans, 128), F32)]
    params = [conv_reduce.swapaxes(1, 2), conv_spatial, conv_expand, scale_mid, shift_mid, scale_out, shift_out]

    def small(count):
        return (count, mid, cols), BF16

    def large(count):
        return (count, chans, cols), BF16

    inner, edge = rows - 2, 2
    row = ((mid, cols), BF16)
    acc_c = ((mid, chans), F32)
    acc_s = ((3 * mid, 3 * mid), F32)

    wr, kf, kf2, we, we_back, kb, kb2, wr_back, b1, b2, b3, x0, slope1_0e, top, bottom = call(
        start, [((2,) + s, d) for s, d in made] + [large(rows), small(edge), row, row],
        [heights, widths] + [pltpu.with_memory_space_constraint(a, pltpu.HBM) for a in [images[0]] + params], "start", [SMEM] * 2 + [HBM] * 8,
        scratch=[pltpu.VMEM(p.shape, p.dtype) for p in params] + [pltpu.SemaphoreType.DMA((rows + len(params),))])
    f0a, f0b = exchange(top, bottom)
    hw = [heights, widths]
    fwd = [kf, kf2, b2, we, b3, wr, b1]
    first0, slope1_0i, second0i, slope2_0i, slope3_0i, x1i, slope1_1i, first1i = placed_call(
        forward_inner, [small(rows)] + [small(inner)] * 3 + [large(inner)] * 2 + [small(inner)] * 2,
        hw + [x0, top, bottom] + fwd, "forward_inner")
    second0e, slope2_0e, slope3_0e, x1e, slope1_1e, first1, top, bottom = placed_call(
        forward_edge, [small(edge)] * 2 + [large(edge)] * 2 + [small(edge), small(rows), row, row],
        hw + [x0, first0, f0a, f0b, first1i] + fwd, "forward_edge")
    f1a, f1b = exchange(top, bottom)
    turn = [kf, kf2, b2, we, b3, we_back]
    gsum1i, gmid2_1i, dexp1 = placed_call(
        turn_inner, [large(inner), small(inner), acc_c], hw + [first1, x1i, cot] + turn, "turn_inner")
    gsum1e, gmid2_1, dexp1, top, bottom = placed_call(
        turn_edge, [large(edge), small(rows), acc_c, row, row],
        hw + [first1, f1a, f1b, x1e, cot] + turn + [gmid2_1i, dexp1], "turn_edge")
    g1a, g1b = exchange(top, bottom)
    back = [kb, kb2, wr_back, we_back]
    sums = [acc_c, acc_s, acc_c]
    gsum0i, gmid2_0i, *partial = placed_call(
        backward_inner, [large(inner), small(inner)] + sums,
        hw + [gmid2_1, first1, slope1_1i, x1i, gsum1i, slope3_0i, slope2_0i, second0i] + back, "backward_inner")
    gsum0e, gmid2_0, dred1, dspat1, dexp0, top, bottom = placed_call(
        backward_edge, [large(edge), small(rows)] + sums + [row, row],
        hw + [gmid2_1, g1a, g1b, first1, f1a, f1b, slope1_1e, x1e, gsum1e, slope3_0e, slope2_0e, second0e] + back
        + [gmid2_0i] + partial, "backward_edge")
    g0a, g0b = exchange(top, bottom)
    gmid1_0i, dred0, dspat0 = call(
        last_inner, [small(inner), acc_c, acc_s], [gmid2_0, first0, slope1_0i, x0, kb, kb2], "last_inner")
    gmid1_0e, terms = call(
        last_edge, [small(edge), ((4 * mid + 6 * mid, chans), BF16)],
        [gmid2_0, g0a, g0b, first0, f0a, f0b, slope1_0e, x0, kb, kb2, dred0, dspat0, dred1, dexp0, dexp1, dspat1],
        "last_edge", scratch=[pltpu.VMEM(*acc_c), pltpu.VMEM(*acc_s)])
    (grad,) = call(
        grad_rows, [large(rows)], [gmid1_0i, gmid1_0e, gsum0i, gsum0e, wr_back], "grad_images", out_specs=[HBM],
        scratch=[pltpu.VMEM(*large(rows)), pltpu.SemaphoreType.DMA((rows,))])
    summed = all_sum(terms)
    factor = 1.0 / math.sqrt(lax.axis_size("batch") * rows * lax.axis_size("space") * cols)
    g_reduce, g_spatial, g_expand = call(
        functools.partial(finish, factor),
        [((2, mid, chans), F32), (conv_spatial.shape, F32), ((2, mid, chans), F32)], [summed, scale_out], "finish")
    return grad[None], g_reduce.swapaxes(1, 2), g_spatial, g_expand


def solution(mesh):
    strips = P("batch", "space", None, None)
    placed = (strips, P("batch"), P("batch")) + (P(),) * 7 + (strips,)
    return jax.shard_map(
        body, mesh=mesh, in_specs=placed, out_specs=(strips, P(), P(), P()), check_vma=False)
```

```python
import functools
import math

import jax
import jax.numpy as jnp
from jax import lax
from jax.experimental import pallas as pl
from jax.experimental.pallas import tpu as pltpu
from jax.sharding import PartitionSpec as P

F32 = jnp.float32
BF16 = jnp.bfloat16
VMEM_LIMIT = 12 * 1024 * 1024
VMEM = pl.BlockSpec(memory_space=pltpu.VMEM)
SMEM = pl.BlockSpec(memory_space=pltpu.SMEM)
HBM = pl.BlockSpec(memory_space=pltpu.HBM)


def mm(a, b):
    return lax.dot_general(a, b, (((1,), (0,)), ((), ())), preferred_element_type=F32)


def mm_nt(a, b):
    return lax.dot_general(a, b, (((1,), (1,)), ((), ())), preferred_element_type=F32)


def gate(h):
    t = jnp.tanh(h)
    p = 1 + t
    y = h * p
    return y, p + y * (1 - t)


def wide(bias, cols):
    return jnp.concatenate([bias[...]] * (cols // bias.shape[-1]), axis=1)


def row_mask(heights, widths, row, rows, cols):
    where = lax.axis_index("space") * rows + row
    limit = jnp.where(where < heights[0], widths[0], 0)
    ids = lax.broadcasted_iota(jnp.int32, (1, cols), 1)
    return jnp.where(ids < limit, 1.0, 0.0).astype(BF16)


def before(v):
    ids = lax.broadcasted_iota(jnp.int32, (1, v.shape[-1]), 1)
    return pltpu.roll(v, 1, 1) * jnp.where(ids > 0, 1.0, 0.0).astype(v.dtype)


def after(v):
    cols = v.shape[-1]
    ids = lax.broadcasted_iota(jnp.int32, (1, cols), 1)
    return pltpu.roll(v, cols - 1, 1) * jnp.where(ids < cols - 1, 1.0, 0.0).astype(v.dtype)


def edge_taps(strip, halo_above, halo_below, last):
    me = lax.axis_index("space")
    rows = strip.shape[0]
    if last:
        have = jnp.where(me < lax.axis_size("space") - 1, 1.0, 0.0).astype(BF16)
        parts = [strip[rows - 2], strip[rows - 1], halo_below[...] * have]
    else:
        have = jnp.where(me > 0, 1.0, 0.0).astype(BF16)
        parts = [halo_above[...] * have, strip[0], strip[1]]
    return jnp.concatenate(parts, axis=0)


def inner_taps(strip, row, count):
    part = strip[pl.ds(row - 1, count)]
    return part.reshape(part.shape[0] * part.shape[1], part.shape[2])


def join(out, flip):
    mid = out.shape[0] // 3
    first, centre, last = out[:mid], out[mid : 2 * mid], out[2 * mid :]
    if flip:
        first, last = last, first
    return before(first) + centre + after(last)


def spread(v):
    return jnp.concatenate([after(v), v, before(v)], axis=0)


def chunks(cols, count=1):
    return [slice(c, c + cols // count) for c in range(0, cols, cols // count)]


def reduce_part(x, w_reduce, b_first, mask):
    h = (mm(w_reduce[...], x) + wide(b_first, x.shape[-1])).astype(BF16)
    y, d = gate(h)
    return y * mask, d * mask


def conv_rows(edges, rows, strip, halos, single, double, flip, work):
    if edges:
        for last in (False, True):
            taps = edge_taps(strip, *halos, last)
            work(rows - 1 if last else 0, int(last), join(mm(single[...], taps), flip))
        return

    def pair(i, carry):
        row = 1 + 2 * i
        out = mm(double[...], inner_taps(strip, row, 4))
        half = out.shape[0] // 2
        work(row, row - 1, join(out[:half], flip))
        work(row + 1, row, join(out[half:], flip))
        return carry

    lax.fori_loop(0, (rows - 2) // 2, pair, 0)


def taps_of(edges, strip, halos, row):
    return edge_taps(strip, *halos, row > 0) if edges else inner_taps(strip, row, 3)


def start_sums(have, sums):
    for value, out in zip(have or [None] * len(sums), sums):
        out[...] = jnp.zeros_like(out) if value is None else value[...]


def gather_rows(full, inner, top, bottom):
    rows = full.shape[0]
    full[0] = top[...]
    full[rows - 1] = bottom[...]
    for r in range(1, rows - 1):
        full[r] = inner[r - 1]


def forward_rows(edges, hw, strip, halos, x, kf, kf2, b_second, we, b_out, w_reduce, b_first,
                 second, slope2, slope3, x1, slope1, put_first):
    rows, cols = x.shape[0], x.shape[-1]

    def work(row, slot, pre):
        mask = row_mask(*hw, row, rows, cols)
        for cut in chunks(cols):
            h = (pre[:, cut] + wide(b_second, cols)).astype(BF16)
            y, d = gate(h)
            second[slot, :, cut] = y
            slope2[slot, :, cut] = d
            h = (mm(we[...], y) + wide(b_out, cols)).astype(BF16) + x[row, :, cut] * 0.5
            y, d = gate(h)
            slope3[slot, :, cut] = d
            x1[slot, :, cut] = y
            first, slope1[slot, :, cut] = reduce_part(y, w_reduce, b_first, mask[:, cut])
            put_first(row, slot, cut, first)

    conv_rows(edges, rows, strip, halos, kf, kf2, False, work)


def forward_inner(heights, widths, x, top, bottom, kf, kf2, b2, we, b3, wr, b1,
                  first0, slope1_0, second, slope2, slope3, x1, slope1_1, first1):
    rows, cols = x.shape[0], x.shape[-1]
    first0[0] = top[...]
    first0[rows - 1] = bottom[...]

    @pl.loop(1, rows - 1)
    def _(row):
        mask = row_mask(heights, widths, row, rows, cols)
        for cut in chunks(cols):
            first0[row, :, cut], slope1_0[row - 1, :, cut] = reduce_part(
                x[row, :, cut], wr.at[0], b1.at[0], mask[:, cut])

    def put_first(row, slot, cut, value):
        first1[slot, :, cut] = value

    forward_rows(False, (heights, widths), first0, None, x, kf.at[0], kf2.at[0], b2.at[0], we.at[0], b3.at[0],
                 wr.at[1], b1.at[1], second, slope2, slope3, x1, slope1_1, put_first)


def forward_edge(heights, widths, x, first0, above, below, first1_inner, kf, kf2, b2, we, b3, wr, b1,
                 second, slope2, slope3, x1, slope1_1, first1, top, bottom):
    def put_first(row, slot, cut, value):
        (bottom if slot else top)[:, cut] = value

    forward_rows(True, (heights, widths), first0, (above, below), x, kf.at[0], kf2.at[0], b2.at[0], we.at[0],
                 b3.at[0], wr.at[1], b1.at[1], second, slope2, slope3, x1, slope1_1, put_first)
    gather_rows(first1, first1_inner, top, bottom)


def turn_rows(edges, hw, first1, halos, x1, cot, kf, kf2, b2, we, b3, we_back, gsum, dexp, put_mid2):
    rows, cols = cot.shape[0], cot.shape[-1]

    def work(row, slot, pre):
        mask = row_mask(*hw, row, rows, cols)
        for cut in chunks(cols, 2):
            h = (pre[:, cut] + wide(b2.at[1], cols // 2)).astype(BF16)
            y2, d2 = gate(h)
            h = (mm(we[1], y2) + wide(b3.at[1], cols // 2)).astype(BF16) + x1[slot, :, cut] * 0.5
            _, d3 = gate(h)
            g = cot[row, :, cut] * mask[:, cut] * d3
            gsum[slot, :, cut] = g
            put_mid2(row, slot, cut, mm(we_back[1], g).astype(BF16) * d2)
            dexp[...] += mm_nt(y2, g)

    conv_rows(edges, rows, first1, halos, kf.at[1], kf2.at[1], False, work)


def turn_inner(heights, widths, first1, x1, cot, kf, kf2, b2, we, b3, we_back, gsum, gmid2, dexp):
    start_sums(None, [dexp])

    def put_mid2(row, slot, cut, value):
        gmid2[slot, :, cut] = value

    turn_rows(False, (heights, widths), first1, None, x1, cot, kf, kf2, b2, we, b3, we_back, gsum, dexp, put_mid2)


def turn_edge(heights, widths, first1, above, below, x1, cot, kf, kf2, b2, we, b3, we_back, gmid2_inner, dexp_inner,
              gsum, gmid2, dexp, top, bottom):
    start_sums([dexp_inner], [dexp])

    def put_mid2(row, slot, cut, value):
        (bottom if slot else top)[:, cut] = value

    turn_rows(True, (heights, widths), first1, (above, below), x1, cot, kf, kf2, b2, we, b3, we_back, gsum, dexp, put_mid2)
    gather_rows(gmid2, gmid2_inner, top, bottom)


def backward_rows(edges, hw, gmid2, g_halos, first1, f_halos, slope1, x1, gsum1, slope3, slope2, second,
                  kb, kb2, wr_back, we_back, gsum0, dred, dspat, dexp, put_mid2):
    rows, cols = gmid2.shape[0], gmid2.shape[-1]

    def work(row, slot, back):
        mask = row_mask(*hw, row, rows, cols)
        for cut in chunks(cols):
            g1 = back[:, cut].astype(BF16) * slope1[slot, :, cut]
            dred[...] += mm_nt(g1, x1[slot, :, cut])
            up = (mm(wr_back[1], g1) + gsum1[slot, :, cut].astype(F32)).astype(BF16)
            g = up * slope3[slot, :, cut] * mask[:, cut]
            gsum0[slot, :, cut] = g
            put_mid2(row, slot, cut, mm(we_back[0], g).astype(BF16) * slope2[slot, :, cut])
            dexp[...] += mm_nt(second[slot, :, cut], g)
        dspat[...] += mm_nt(taps_of(edges, first1, f_halos, row), spread(gmid2[row]))

    conv_rows(edges, rows, gmid2, g_halos, kb.at[1], kb2.at[1], True, work)


def backward_inner(heights, widths, gmid2, first1, slope1, x1, gsum1, slope3, slope2, second, kb, kb2, wr_back, we_back,
                   gsum0, gmid2_0, dred, dspat, dexp):
    start_sums(None, [dred, dspat, dexp])

    def put_mid2(row, slot, cut, value):
        gmid2_0[slot, :, cut] = value

    backward_rows(False, (heights, widths), gmid2, None, first1, None, slope1, x1, gsum1, slope3, slope2, second,
                  kb, kb2, wr_back, we_back, gsum0, dred, dspat, dexp, put_mid2)


def backward_edge(heights, widths, gmid2, above, below, first1, f_above, f_below, slope1, x1, gsum1, slope3, slope2, second,
                  kb, kb2, wr_back, we_back, gmid2_inner, dred_inner, dspat_inner, dexp_inner,
                  gsum0, gmid2_0, dred, dspat, dexp, top, bottom):
    start_sums([dred_inner, dspat_inner, dexp_inner], [dred, dspat, dexp])

    def put_mid2(row, slot, cut, value):
        (bottom if slot else top)[:, cut] = value

    backward_rows(True, (heights, widths), gmid2, (above, below), first1, (f_above, f_below), slope1, x1, gsum1, slope3,
                  slope2, second, kb, kb2, wr_back, we_back, gsum0, dred, dspat, dexp, put_mid2)
    gather_rows(gmid2_0, gmid2_inner, top, bottom)


def last_rows(edges, gmid2, g_halos, first0, f_halos, slope1, x, kb, kb2, gmid1, dred, dspat):
    def work(row, slot, back):
        g1 = back.astype(BF16) * slope1[slot]
        gmid1[slot] = g1
        dred[...] += mm_nt(g1, x[row])
        dspat[...] += mm_nt(taps_of(edges, first0, f_halos, row), spread(gmid2[row]))

    conv_rows(edges, x.shape[0], gmid2, g_halos, kb.at[0], kb2.at[0], True, work)


def last_inner(gmid2, first0, slope1, x, kb, kb2, gmid1, dred, dspat):
    start_sums(None, [dred, dspat])
    last_rows(False, gmid2, None, first0, None, slope1, x, kb, kb2, gmid1, dred, dspat)


def last_edge(gmid2, above, below, first0, f_above, f_below, slope1, x, kb, kb2, dred_inner, dspat_inner,
              dred1, dexp0, dexp1, dspat1, gmid1, terms, dred, dspat):
    start_sums([dred_inner, dspat_inner], [dred, dspat])
    last_rows(True, gmid2, (above, below), first0, (f_above, f_below), slope1, x, kb, kb2, gmid1, dred, dspat)
    at = 0
    for value in (dred, dred1, dexp0, dexp1, dspat, dspat1):
        tall, across = value.shape
        terms[at : at + tall, :across] = value[...].astype(BF16)
        if across < terms.shape[1]:
            terms[at : at + tall, across:] = jnp.zeros((tall, terms.shape[1] - across), BF16)
        at += tall


def grad_rows(gmid1_inner, gmid1_edge, gsum_inner, gsum_edge, wr_back, out, held, sems):
    rows, cols = held.shape[0], held.shape[-1]

    def work(row, slot, gmid1, gsum):
        for cut in chunks(cols):
            acc = mm(wr_back[0], gmid1[slot, :, cut]) + gsum[slot, :, cut].astype(F32) * 0.25
            held[row, :, cut] = acc.astype(BF16)
        pltpu.make_async_copy(held.at[row], out.at[row], sems.at[row]).start()

    @pl.loop(1, rows - 1)
    def _(row):
        work(row, row - 1, gmid1_inner, gsum_inner)

    work(0, 0, gmid1_edge, gsum_edge)
    work(rows - 1, 1, gmid1_edge, gsum_edge)
    for r in range(rows):
        pltpu.make_async_copy(held.at[r], out.at[r], sems.at[r]).wait()


def finish(factor, terms, scale_out, g_reduce, g_spatial, g_expand):
    mid = g_reduce.shape[1]
    for k in range(2):
        g_reduce[k] = terms[k * mid : (k + 1) * mid].astype(F32) * factor
        scale = scale_out[k : k + 1, :] * (factor * 0.5 ** (2 - k))
        g_expand[k] = terms[(2 + k) * mid : (3 + k) * mid].astype(F32) * scale
        base = (4 + 3 * k) * mid
        for a in range(3):
            for b in range(3):
                part = terms[base + a * mid : base + (a + 1) * mid, b * mid : (b + 1) * mid]
                g_spatial[k, a, b] = part.astype(F32) * factor


def lanes(vector, count):
    return jnp.broadcast_to(vector, (count, vector.shape[-1])).T


def start(heights, widths, images, red_h, spa_h, exp_h, sm_h, sh_h, so_h, sho_h,
          wr, kf, kf2, we, we_back, kb, kb2, wr_back, b1, b2, b3, x, slope1, top, bottom,
          red, spa, exp, scale_mid, shift_mid, scale_out, shift_out, sems):
    rows, cols = x.shape[0], x.shape[-1]
    params = list(zip((red_h, spa_h, exp_h, sm_h, sh_h, so_h, sho_h),
                      (red, spa, exp, scale_mid, shift_mid, scale_out, shift_out)))
    small = [pltpu.make_async_copy(s, d, sems.at[rows + n]) for n, (s, d) in enumerate(params)]
    strips = [pltpu.make_async_copy(images.at[r], x.at[r], sems.at[r]) for r in range(rows)]
    for copy in small:
        copy.start()
    for r in (0, rows - 1, *range(1, rows - 1)):
        strips[r].start()
    for copy in small:
        copy.wait()
    mid = red.shape[1]
    kf2[...] = jnp.zeros_like(kf2)
    kb2[...] = jnp.zeros_like(kb2)
    for k in range(2):
        twice = 2.0 ** (2 - k)
        s1, s2 = scale_mid[k, 0:1, :], scale_mid[k, 1:2, :]
        so = scale_out[k : k + 1, :]
        r, e = red[k].astype(F32), exp[k].astype(F32)
        chans = r.shape[-1]
        wr[k] = (r * (0.5 * lanes(s1, chans))).astype(BF16)
        wr_back[k] = (r * (1.0 if k == 0 else twice)).T.astype(BF16)
        we[k] = (e * (0.5 * so)).T.astype(BF16)
        we_back[k] = (e * (so * (0.5 / twice)) * lanes(s2, chans)).astype(BF16)
        half = 0.5 * lanes(s1, mid)
        for a in range(3):
            for b in range(3):
                part = spa[k, a, b].astype(F32)
                ahead = (part * (0.5 * s2)).T.astype(BF16)
                back = (part * half).astype(BF16)
                for out, out2, value, at in ((kf, kf2, ahead, a), (kb, kb2, back, 2 - a)):
                    out[k, b * mid : (b + 1) * mid, at * mid : (at + 1) * mid] = value
                    for j in range(2):
                        out2[k, (3 * j + b) * mid : (3 * j + b + 1) * mid, (at + j) * mid : (at + j + 1) * mid] = value
        b1[k] = 0.5 * lanes(shift_mid[k, 0:1, :], b1.shape[-1])
        b2[k] = 0.5 * lanes(shift_mid[k, 1:2, :], b2.shape[-1])
        b3[k] = 0.5 * lanes(shift_out[k : k + 1, :], b3.shape[-1])
    for slot, (row, edge) in enumerate(((0, top), (rows - 1, bottom))):
        strips[row].wait()
        mask = row_mask(heights, widths, row, rows, cols)
        for cut in chunks(cols):
            edge[:, cut], slope1[slot, :, cut] = reduce_part(x[row, :, cut], wr.at[0], b1.at[0], mask[:, cut])
    for r in range(1, rows - 1):
        strips[r].wait()


def call(kernel, outs, args, name, specs=None, out_specs=None, scratch=(), limit=VMEM_LIMIT):
    return pl.pallas_call(
        kernel,
        in_specs=specs or [VMEM] * len(args),
        out_specs=out_specs or [VMEM] * len(outs),
        out_shape=[jax.ShapeDtypeStruct(s, d) for s, d in outs],
        scratch_shapes=list(scratch),
        compiler_params=pltpu.CompilerParams(vmem_limit_bytes=limit),
        name=name,
    )(*args)


def placed_call(kernel, outs, args, name):
    return call(kernel, outs, args, name, [SMEM] * 2 + [VMEM] * (len(args) - 2))


def exchange(top, bottom):
    count = lax.axis_size("space")
    above = lax.ppermute(bottom, "space", [(i, (i + 1) % count) for i in range(count)])
    below = lax.ppermute(top, "space", [((i + 1) % count, i) for i in range(count)])
    return above, below


def all_sum(terms, beside):
    n = lax.axis_size("batch")
    tall, across = terms.shape
    shares = lax.all_to_all(terms.reshape(n, tall // n, across), "batch", 0, 0, tiled=True)
    share = shares.astype(F32).sum(0)
    count = lax.axis_size("space")
    for bit in (2, 6, 1):
        share = share + lax.ppermute(share.astype(BF16), "space", [(i, i ^ bit) for i in range(count)]).astype(F32)
    spread_out = jnp.broadcast_to(share.astype(BF16)[None], (n,) + share.shape)
    spread_out, beside = lax.optimization_barrier((spread_out, beside))
    return lax.all_to_all(spread_out, "batch", 0, 0, tiled=True).reshape(terms.shape), beside


def body(images, heights, widths, conv_reduce, conv_spatial, conv_expand, scale_mid, shift_mid,
         scale_out, shift_out, cotangent):
    _, rows, chans, cols = images.shape
    mid = conv_reduce.shape[-1]
    cot = cotangent[0]
    wide_w, tall_w = ((mid, chans), BF16), ((chans, mid), BF16)
    single, double = ((3 * mid, 3 * mid), BF16), ((6 * mid, 4 * mid), BF16)
    bias = ((mid, 128), F32)
    made = [wide_w, single, double, tall_w, wide_w, single, double, tall_w, bias, bias, ((chans, 128), F32)]
    params = [conv_reduce.swapaxes(1, 2), conv_spatial, conv_expand, scale_mid, shift_mid, scale_out, shift_out]

    def small(count):
        return (count, mid, cols), BF16

    def large(count):
        return (count, chans, cols), BF16

    inner, edge = rows - 2, 2
    row = ((mid, cols), BF16)
    acc_c = ((mid, chans), F32)
    acc_s = ((3 * mid, 3 * mid), F32)

    wr, kf, kf2, we, we_back, kb, kb2, wr_back, b1, b2, b3, x0, slope1_0e, top, bottom = call(
        start, [((2,) + s, d) for s, d in made] + [large(rows), small(edge), row, row],
        [heights, widths] + [pltpu.with_memory_space_constraint(a, pltpu.HBM) for a in [images[0]] + params], "start", [SMEM] * 2 + [HBM] * 8,
        scratch=[pltpu.VMEM(p.shape, p.dtype) for p in params] + [pltpu.SemaphoreType.DMA((rows + len(params),))])
    f0a, f0b = exchange(top, bottom)
    hw = [heights, widths]
    fwd = [kf, kf2, b2, we, b3, wr, b1]
    first0, slope1_0i, second0i, slope2_0i, slope3_0i, x1i, slope1_1i, first1i = placed_call(
        forward_inner, [small(rows)] + [small(inner)] * 3 + [large(inner)] * 2 + [small(inner)] * 2,
        hw + [x0, top, bottom] + fwd, "forward_inner")
    second0e, slope2_0e, slope3_0e, x1e, slope1_1e, first1, top, bottom = placed_call(
        forward_edge, [small(edge)] * 2 + [large(edge)] * 2 + [small(edge), small(rows), row, row],
        hw + [x0, first0, f0a, f0b, first1i] + fwd, "forward_edge")
    f1a, f1b = exchange(top, bottom)
    turn = [kf, kf2, b2, we, b3, we_back]
    gsum1i, gmid2_1i, dexp1 = placed_call(
        turn_inner, [large(inner), small(inner), acc_c], hw + [first1, x1i, cot] + turn, "turn_inner")
    gsum1e, gmid2_1, dexp1, top, bottom = placed_call(
        turn_edge, [large(edge), small(rows), acc_c, row, row],
        hw + [first1, f1a, f1b, x1e, cot] + turn + [gmid2_1i, dexp1], "turn_edge")
    g1a, g1b = exchange(top, bottom)
    back = [kb, kb2, wr_back, we_back]
    sums = [acc_c, acc_s, acc_c]
    gsum0i, gmid2_0i, *partial = placed_call(
        backward_inner, [large(inner), small(inner)] + sums,
        hw + [gmid2_1, first1, slope1_1i, x1i, gsum1i, slope3_0i, slope2_0i, second0i] + back, "backward_inner")
    gsum0e, gmid2_0, dred1, dspat1, dexp0, top, bottom = placed_call(
        backward_edge, [large(edge), small(rows)] + sums + [row, row],
        hw + [gmid2_1, g1a, g1b, first1, f1a, f1b, slope1_1e, x1e, gsum1e, slope3_0e, slope2_0e, second0e] + back
        + [gmid2_0i] + partial, "backward_edge")
    g0a, g0b = exchange(top, bottom)
    gmid1_0i, dred0, dspat0 = call(
        last_inner, [small(inner), acc_c, acc_s], [gmid2_0, first0, slope1_0i, x0, kb, kb2], "last_inner")
    gmid1_0e, terms = call(
        last_edge, [small(edge), ((4 * mid + 6 * mid, chans), BF16)],
        [gmid2_0, g0a, g0b, first0, f0a, f0b, slope1_0e, x0, kb, kb2, dred0, dspat0, dred1, dexp0, dexp1, dspat1],
        "last_edge", scratch=[pltpu.VMEM(*acc_c), pltpu.VMEM(*acc_s)])
    (grad,) = call(
        grad_rows, [large(rows)], [gmid1_0i, gmid1_0e, gsum0i, gsum0e, wr_back], "grad_images", out_specs=[HBM],
        scratch=[pltpu.VMEM(*large(rows)), pltpu.SemaphoreType.DMA((rows,))])
    summed, grad = all_sum(terms, grad)
    factor = 1.0 / math.sqrt(lax.axis_size("batch") * rows * lax.axis_size("space") * cols)
    g_reduce, g_spatial, g_expand = call(
        functools.partial(finish, factor),
        [((2, mid, chans), F32), (conv_spatial.shape, F32), ((2, mid, chans), F32)], [summed, scale_out], "finish")
    return grad[None], g_reduce.swapaxes(1, 2), g_spatial, g_expand


def solution(mesh):
    strips = P("batch", "space", None, None)
    placed = (strips, P("batch"), P("batch")) + (P(),) * 7 + (strips,)
    return jax.shard_map(
        body, mesh=mesh, in_specs=placed, out_specs=(strips, P(), P(), P()), check_vma=False)
```

```python
import functools
import math

import jax
import jax.numpy as jnp
from jax import lax
from jax.experimental import pallas as pl
from jax.experimental.pallas import tpu as pltpu
from jax.sharding import PartitionSpec as P

F32 = jnp.float32
BF16 = jnp.bfloat16
VMEM_LIMIT = 12 * 1024 * 1024
BESIDE = 2
VMEM = pl.BlockSpec(memory_space=pltpu.VMEM)
HBM = pl.BlockSpec(memory_space=pltpu.HBM)


def mm(a, b):
    return lax.dot_general(a, b, (((1,), (0,)), ((), ())), preferred_element_type=F32)


def mm_nt(a, b):
    return lax.dot_general(a, b, (((1,), (1,)), ((), ())), preferred_element_type=F32)


def gate(h):
    t = jnp.tanh(h)
    p = 1 + t
    y = h * p
    return y.astype(BF16), (p + y * (1 - t)).astype(BF16)


def wide(bias, cols):
    return jnp.concatenate([bias[...]] * (cols // bias.shape[-1]), axis=1)


def row_mask(limits, row, cols):
    limit = jnp.concatenate([limits[row : row + 1, :]] * (cols // limits.shape[1]), axis=1)
    ids = lax.broadcasted_iota(jnp.int32, (1, cols), 1)
    return jnp.where(ids < limit, 1.0, 0.0).astype(BF16)


def inside(mask, row, chans):
    return jnp.concatenate([mask[row]] * (chans // mask.shape[1]), axis=0)


def before(v):
    v = pltpu.roll(v, 1, 1)
    ids = lax.broadcasted_iota(jnp.int32, (1, 128), 1)
    edge = v[:, :128] * jnp.where(ids > 0, 1.0, 0.0).astype(v.dtype)
    return jnp.concatenate([edge, v[:, 128:]], axis=1)


def after(v):
    cols = v.shape[-1]
    v = pltpu.roll(v, cols - 1, 1)
    ids = lax.broadcasted_iota(jnp.int32, (1, 128), 1)
    edge = v[:, cols - 128 :] * jnp.where(ids < 127, 1.0, 0.0).astype(v.dtype)
    return jnp.concatenate([v[:, : cols - 128], edge], axis=1)


def edge_taps(strip, halo_above, halo_below, last):
    me = lax.axis_index("space")
    rows = strip.shape[0]
    if last:
        have = jnp.where(me < lax.axis_size("space") - 1, 1.0, 0.0).astype(BF16)
        parts = [strip[rows - 2], strip[rows - 1], halo_below[...] * have]
    else:
        have = jnp.where(me > 0, 1.0, 0.0).astype(BF16)
        parts = [halo_above[...] * have, strip[0], strip[1]]
    return jnp.concatenate(parts, axis=0)


def inner_taps(strip, row, count):
    part = strip[pl.ds(row - 1, count)]
    return part.reshape(part.shape[0] * part.shape[1], part.shape[2])


def join(out, flip):
    mid = out.shape[0] // 3
    first, centre, last = out[:mid], out[mid : 2 * mid], out[2 * mid :]
    if flip:
        first, last = last, first
    return before(first) + centre + after(last)


def spread(v):
    return jnp.concatenate([after(v), v, before(v)], axis=0)


def chunks(cols, count=1):
    return [slice(c, c + cols // count) for c in range(0, cols, cols // count)]


def reduce_part(x, w_reduce, b_first, mask):
    h = mm(w_reduce[...], x) + wide(b_first, x.shape[-1])
    y, d = gate(h)
    return y * mask, d * mask


def conv_rows(edges, rows, strip, halos, single, double, flip, work, unroll=True):
    if edges:
        ends = [mm(single[...], edge_taps(strip, *halos, last)) for last in (False, True)]
        work([(0, 0, join(ends[0], flip)), (rows - 1, 1, join(ends[1], flip))])
        return

    def pair(i, carry):
        row = 1 + 2 * i
        out = mm(double[...], inner_taps(strip, row, 4))
        half = out.shape[0] // 2
        work([(row, row - 1, join(out[:half], flip)), (row + 1, row, join(out[half:], flip))])
        return carry

    lax.fori_loop(0, (rows - 2) // 2, pair, 0, unroll=unroll)


def both(weights, pair):
    out = mm(weights, jnp.concatenate(pair, axis=0))
    half = out.shape[0] // 2
    return out[:half], out[half:]


def mm_nt_sum(pairs):
    return mm_nt(*(jnp.concatenate(side, axis=1) for side in zip(*pairs)))


def tap_terms(first, gmid2, rows):
    return mm_nt_sum([(inner_taps(first, row, 3), spread(gmid2[row])) for row in rows])


def edge_tap_terms(first, halos, gmid2):
    ends = ((False, 0), (True, first.shape[0] - 1))
    return mm_nt_sum([(edge_taps(first, *halos, last), spread(gmid2[row])) for last, row in ends])


def start_sums(have, sums):
    for value, out in zip(have or [None] * len(sums), sums):
        out[...] = jnp.zeros_like(out) if value is None else value[...]


def gather_rows(full, inner, top, bottom):
    rows = full.shape[0]
    full[0] = top[...]
    full[rows - 1] = bottom[...]
    for r in range(1, rows - 1):
        full[r] = inner[r - 1]


def forward_rows(edges, mask, rows, strip, halos, x, kf, kf2, b_second, we, b_out, w_reduce, b_first,
                 second, slope2, slope3, x1, slope1, put_first):
    cols = x.shape[-1]

    def work(pair):
        seconds = []
        for _, slot, pre in pair:
            y, d = gate(pre + wide(b_second, cols))
            second[slot] = y
            slope2[slot] = d
            seconds.append(y)
        for (row, slot, _), expanded in zip(pair, both(we[...], seconds)):
            y, d = gate(expanded + wide(b_out, cols) + x[row].astype(F32) * 0.5)
            slope3[slot] = d
            x1[slot] = y
            first, slope1[slot] = reduce_part(y, w_reduce, b_first, inside(mask, row, slope1.shape[1]))
            put_first(row, slot, first)

    conv_rows(edges, rows, strip, halos, kf, kf2, False, work)


def forward_inner(mask, x, top, bottom, wr_0, b1_0, red, spa, exp, scale_mid, shift_mid, scale_out, shift_out,
                  first0, slope1_0, second, slope2, slope3, x1, slope1_1, first1,
                  wr, kf, kf2, we, we_back, kb, kb2, wr_back, b1, b2, b3):
    rows, cols = x.shape[0], x.shape[-1]
    prepare(red, spa, exp, scale_mid, shift_mid, scale_out, shift_out, wr, kf, kf2, we, we_back, kb, kb2, wr_back, b1, b2, b3)
    first0[0] = top[...]
    first0[rows - 1] = bottom[...]

    @pl.loop(1, rows - 1, unroll=True)
    def _(row):
        first0[row], slope1_0[row - 1] = reduce_part(x[row], wr_0, b1_0, inside(mask, row, first0.shape[1]))

    def put_first(row, slot, value):
        first1[slot] = value

    forward_rows(False, mask, rows, first0, None, x, kf.at[0], kf2.at[0], b2.at[0], we.at[0], b3.at[0],
                 wr, b1, second, slope2, slope3, x1, slope1_1, put_first)


def forward_edge(mask, x, first0, above, below, first1_inner, kf, kf2, b2, we, b3, wr, b1,
                 second, slope2, slope3, x1, slope1_1, first1, top, bottom):
    def put_first(row, slot, value):
        (bottom if slot else top)[...] = value

    forward_rows(True, mask, first0.shape[0], first0, (above, below), x, kf.at[0], kf2.at[0], b2.at[0], we.at[0],
                 b3.at[0], wr, b1, second, slope2, slope3, x1, slope1_1, put_first)
    gather_rows(first1, first1_inner, top, bottom)


def turn_rows(edges, mask, first1, halos, x1, cot, kf, kf2, b2, we, b3, we_back, gsum, dexp, put_mid2, second=None):
    rows, cols = cot.shape[0], cot.shape[-1]

    def work(pair):
        gates = [gate(pre + wide(b2.at[1], cols)) for _, _, pre in pair]
        expanded = both(we[1], [y2 for y2, _ in gates])
        terms = []
        for (row, slot, _), (y2, d2), pre3 in zip(pair, gates, expanded):
            _, d3 = gate(pre3 + wide(b3.at[1], cols) + x1[slot].astype(F32) * 0.5)
            g = cot[row] * inside(mask, row, cot.shape[1]) * d3
            gsum[slot] = g
            put_mid2(row, slot, mm(we_back[1], g).astype(BF16) * d2)
            terms.append((y2, g))
            if edges:
                second[slot] = y2
        if not edges:
            dexp[...] += mm_nt_sum(terms)

    conv_rows(edges, rows, first1, halos, kf.at[1], kf2.at[1], False, work)


def turn_inner(mask, first1, x1, cot, kf, kf2, b2, we, b3, we_back, gsum, gmid2, dexp):
    start_sums(None, [dexp])

    def put_mid2(row, slot, value):
        gmid2[slot] = value

    turn_rows(False, mask, first1, None, x1, cot, kf, kf2, b2, we, b3, we_back, gsum, dexp, put_mid2)


def turn_edge(mask, first1, above, below, x1, cot, kf, kf2, b2, we, b3, we_back, gmid2_inner,
              gsum, gmid2, second, top, bottom):

    def put_mid2(row, slot, value):
        (bottom if slot else top)[...] = value

    turn_rows(True, mask, first1, (above, below), x1, cot, kf, kf2, b2, we, b3, we_back, gsum, None, put_mid2, second)
    gather_rows(gmid2, gmid2_inner, top, bottom)


def backward_rows(edges, mask, gmid2, g_halos, first1, slope1, x1, gsum1, slope3, slope2,
                  kb, kb2, wr_back, we_back, gsum0, dred, dspat, put_mid2):
    rows, cols = gmid2.shape[0], gmid2.shape[-1]

    def work(pair):
        firsts = [back.astype(BF16) * slope1[slot] for _, slot, back in pair]
        dred[...] += mm_nt_sum([(g1, x1[slot]) for g1, (_, slot, _) in zip(firsts, pair)])
        if not edges:
            dspat[...] += tap_terms(first1, gmid2, [row for row, _, _ in pair])
        ups = both(wr_back[1], firsts)
        for (row, slot, _), g1, up in zip(pair, firsts, ups):
            g = (up + gsum1[slot].astype(F32)).astype(BF16) * slope3[slot] * inside(mask, row, slope3.shape[1])
            gsum0[slot] = g
            put_mid2(row, slot, mm(we_back[0], g).astype(BF16) * slope2[slot])

    conv_rows(edges, rows, gmid2, g_halos, kb.at[1], kb2.at[1], True, work)


def backward_inner(mask, gmid2, first1, f_above, f_below, second_edge, gsum_edge, dexp_turn, slope1, x1, gsum1, slope3, slope2, kb, kb2, wr_back, we_back,
                   gsum0, gmid2_0, dred, dspat, dexp):
    start_sums(None, [dred])
    dspat[...] = edge_tap_terms(first1, (f_above, f_below), gmid2)
    dexp[...] = dexp_turn[...] + mm_nt_sum([(second_edge[n], gsum_edge[n]) for n in range(2)])

    def put_mid2(row, slot, value):
        gmid2_0[slot] = value

    backward_rows(False, mask, gmid2, None, first1, slope1, x1, gsum1, slope3, slope2,
                  kb, kb2, wr_back, we_back, gsum0, dred, dspat, put_mid2)


def backward_edge(mask, gmid2, above, below, slope1, x1, gsum1, slope3, slope2,
                  kb, kb2, wr_back, we_back, gmid2_inner, dred_inner,
                  gsum0, gmid2_0, dred, top, bottom):
    start_sums([dred_inner], [dred])

    def put_mid2(row, slot, value):
        (bottom if slot else top)[...] = value

    backward_rows(True, mask, gmid2, (above, below), None, slope1, x1, gsum1, slope3,
                  slope2, kb, kb2, wr_back, we_back, gsum0, dred, None, put_mid2)
    gather_rows(gmid2_0, gmid2_inner, top, bottom)


def last_rows(edges, gmid2, g_halos, first0, slope1, x, kb, kb2, gmid1, dred, dspat):
    def work(pair):
        firsts = []
        for row, slot, back in pair:
            g1 = back.astype(BF16) * slope1[slot]
            gmid1[slot] = g1
            firsts.append((g1, x[row]))
        dred[...] += mm_nt_sum(firsts)
        if not edges:
            dspat[...] += tap_terms(first0, gmid2, [row for row, _, _ in pair])

    conv_rows(edges, gmid2.shape[0], gmid2, g_halos, kb.at[0], kb2.at[0], True, work, False)


def last_inner(gmid2, first0, f_above, f_below, slope1, x, second_inner, second_edge, gsum_inner, gsum_edge, kb, kb2,
               gmid1, dred, dspat, dexp):
    start_sums(None, [dred])
    dspat[...] = edge_tap_terms(first0, (f_above, f_below), gmid2)
    dexp[...] = mm_nt(second_edge[0], gsum_edge[0]) + mm_nt(second_edge[1], gsum_edge[1])

    @pl.loop(0, second_inner.shape[0] // 2)
    def _(i):
        dexp[...] += mm_nt_sum([(second_inner[2 * i], gsum_inner[2 * i]), (second_inner[2 * i + 1], gsum_inner[2 * i + 1])])

    last_rows(False, gmid2, None, first0, slope1, x, kb, kb2, gmid1, dred, dspat)


def tap_places(mid):
    places = []
    for n in range(9):
        a, b = divmod(n, 3)
        if n < 8:
            base, at = (2 + n // 4) * mid, n % 4
            places.append((slice(a * mid, (a + 1) * mid), slice(b * mid, (b + 1) * mid),
                           slice(base, base + mid), slice(at * mid, (at + 1) * mid)))
        else:
            part = mid // 4
            for q in range(4):
                places.append((slice(a * mid + q * part, a * mid + (q + 1) * part), slice(b * mid, (b + 1) * mid),
                               slice(4 * mid, 4 * mid + part), slice(q * mid, (q + 1) * mid)))
    return places


def last_edge(gmid2, above, below, slope1, x, kb, kb2, dred_inner, dspat,
              dred1, dexp0, dexp1, dspat1, gmid1, keep, send, dred):
    start_sums([dred_inner], [dred])
    last_rows(True, gmid2, (above, below), None, slope1, x, kb, kb2, gmid1, dred, None)
    core = lax.axis_index("batch") % 2

    def pack(out, reduce_term, expand_term, spatial_term):
        mid = reduce_term.shape[0]
        out[:mid] = reduce_term[...].astype(BF16)
        out[mid : 2 * mid] = expand_term[...].astype(BF16)
        for rows_in, cols_in, rows_out, cols_out in tap_places(mid):
            out[rows_out, cols_out] = spatial_term[rows_in, cols_in].astype(BF16)

    for own in range(2):
        @pl.when(core == own)
        def _():
            blocks = ((dred, dexp0, dspat), (dred1, dexp1, dspat1))
            pack(keep, *blocks[own])
            pack(send, *blocks[1 - own])


def grad_rows(gmid1_inner, gmid1_edge, gsum_inner, gsum_edge, wr_back, out, held, sems):
    rows = held.shape[0]

    def work(at, slots, gmid1, gsum):
        for row, slot, acc in zip(at, slots, both(wr_back[0], [gmid1[slot] for slot in slots])):
            held[row] = (acc + gsum[slot].astype(F32) * 0.25).astype(BF16)
            pltpu.make_async_copy(held.at[row], out.at[row], sems.at[row]).start()

    @pl.loop(0, (rows - 2) // 2, unroll=True)
    def _(i):
        work((2 * i + 1, 2 * i + 2), (2 * i, 2 * i + 1), gmid1_inner, gsum_inner)

    work((0, rows - 1), (0, 1), gmid1_edge, gsum_edge)
    for r in range(rows):
        pltpu.make_async_copy(held.at[r], out.at[r], sems.at[r]).wait()


def finish(factor, mine, other, scale_out, g_reduce, g_spatial, g_expand):
    mid = g_reduce.shape[1]
    core = lax.axis_index("batch") % 2
    for terms, k in ((mine, core), (other, 1 - core)):
        g_reduce[k] = terms[:mid].astype(F32) * factor
        scale = jnp.where(k == 0, scale_out[0:1, :] * (factor * 0.25), scale_out[1:2, :] * (factor * 0.5))
        g_expand[k] = terms[mid : 2 * mid].astype(F32) * scale
        for rows_in, cols_in, rows_out, cols_out in tap_places(mid):
            a, b = rows_in.start // mid, cols_in.start // mid
            part = terms[rows_out, cols_out].astype(F32) * factor
            g_spatial[k, a, b, rows_in.start - a * mid : rows_in.stop - a * mid] = part


def lanes(vector, count):
    return jnp.broadcast_to(vector, (count, vector.shape[-1])).T


def twin(out, k, value):
    tall, across = value.shape
    out[k, :tall, :across] = value
    out[k, tall:, across:] = value


def start(limits, images, red_h, spa_h, exp_h, sm_h, sh_h, so_h, sho_h,
          mask, wr, b1, red, spa, exp, scale_mid, shift_mid, scale_out, shift_out, slope1, top, bottom, x, sems):
    rows, cols = images.shape[0], x.shape[-1]
    copies = [pltpu.make_async_copy(s, d, sems.at[n]) for n, (s, d) in enumerate(
        ((sm_h, scale_mid), (sh_h, shift_mid), (red_h, red), (images.at[0], x.at[0]), (images.at[rows - 1], x.at[1]),
         (spa_h, spa), (exp_h, exp), (so_h, scale_out), (sho_h, shift_out)))]
    for copy in copies:
        copy.start()
    for copy in copies[:3]:
        copy.wait()
    for row in range(rows):
        mask[row] = jnp.broadcast_to(row_mask(limits, row, cols), mask.shape[1:])
    wr[...] = (red[0].astype(F32) * (0.5 * lanes(scale_mid[0, 0:1, :], red.shape[-1]))).astype(BF16)
    b1[...] = 0.5 * lanes(shift_mid[0, 0:1, :], b1.shape[-1])
    for slot, (row, edge) in enumerate(((0, top), (rows - 1, bottom))):
        copies[3 + slot].wait()
        edge[...], slope1[slot] = reduce_part(x[slot], wr, b1, inside(mask, row, edge.shape[0]))
    for copy in copies[5:]:
        copy.wait()


def prepare(red, spa, exp, scale_mid, shift_mid, scale_out, shift_out,
            wr, kf, kf2, we, we_back, kb, kb2, wr_back, b1, b2, b3):
    mid = red.shape[1]
    for out in (kf2, kb2, we, wr_back):
        out[...] = jnp.zeros_like(out)
    for k in range(2):
        twice = 2.0 ** (2 - k)
        s1, s2 = scale_mid[k, 0:1, :], scale_mid[k, 1:2, :]
        so = scale_out[k : k + 1, :]
        r, e = red[k].astype(F32), exp[k].astype(F32)
        chans = r.shape[-1]
        if k == 1:
            wr[...] = (r * (0.5 * lanes(s1, chans))).astype(BF16)
            b1[...] = 0.5 * lanes(shift_mid[k, 0:1, :], b1.shape[-1])
        twin(wr_back, k, (r * (1.0 if k == 0 else twice)).T.astype(BF16))
        twin(we, k, (e * (0.5 * so)).T.astype(BF16))
        we_back[k] = (e * (so * (0.5 / twice)) * lanes(s2, chans)).astype(BF16)
        half = 0.5 * lanes(s1, mid)
        for a in range(3):
            for b in range(3):
                part = spa[k, a, b].astype(F32)
                ahead = (part * (0.5 * s2)).T.astype(BF16)
                back = (part * half).astype(BF16)
                for out, out2, value, at in ((kf, kf2, ahead, a), (kb, kb2, back, 2 - a)):
                    out[k, b * mid : (b + 1) * mid, at * mid : (at + 1) * mid] = value
                    for j in range(2):
                        out2[k, (3 * j + b) * mid : (3 * j + b + 1) * mid, (at + j) * mid : (at + j + 1) * mid] = value
        b2[k] = 0.5 * lanes(shift_mid[k, 1:2, :], b2.shape[-1])
        b3[k] = 0.5 * lanes(shift_out[k : k + 1, :], b3.shape[-1])


def call(kernel, outs, args, name, specs=None, out_specs=None, scratch=(), limit=VMEM_LIMIT):
    return pl.pallas_call(
        kernel,
        in_specs=specs or [VMEM] * len(args),
        out_specs=out_specs or [VMEM] * len(outs),
        out_shape=[jax.ShapeDtypeStruct(s, d) for s, d in outs],
        scratch_shapes=list(scratch),
        compiler_params=pltpu.CompilerParams(vmem_limit_bytes=limit),
        name=name,
    )(*args)


def exchange(top, bottom):
    count = lax.axis_size("space")
    above = lax.ppermute(bottom, "space", [(i, (i + 1) % count) for i in range(count)])
    below = lax.ppermute(top, "space", [((i + 1) % count, i) for i in range(count)])
    return above, below


def swaps():
    def flat(z, x, core, y):
        return ((z % 2 * 4 + x) * 2 + core) * 8 + y * 2 + z // 2

    places = [(z, x, core, y) for z in range(4) for x in range(4) for core in range(2) for y in range(4)]
    orders = ((1, 3, 0), (3, 0, 1))
    steps = []
    for turn in range(3):
        for mirror in (1, 3):
            steps.append([(flat(*at), flat(*(c ^ mirror if n == orders[at[2]][turn] else c for n, c in enumerate(at))))
                          for at in places])
    return steps


def all_sum(keep, send, beside):
    cores = [(i, i ^ 1) for i in range(lax.axis_size("batch"))]
    value = keep.astype(F32) + lax.ppermute(send, "batch", cores).astype(F32)
    for step, pairs in enumerate(swaps()):
        if step == BESIDE:
            value, beside = lax.optimization_barrier((value, beside))
        value = value + lax.ppermute(value.astype(BF16), ("batch", "space"), pairs).astype(F32)
    mine = value.astype(BF16)
    return mine, lax.ppermute(mine, "batch", cores), beside


def body(images, heights, widths, conv_reduce, conv_spatial, conv_expand, scale_mid, shift_mid,
         scale_out, shift_out, cotangent):
    _, rows, chans, cols = images.shape
    mid = conv_reduce.shape[-1]
    cot = cotangent[0]
    wide_w, tall_w = ((mid, chans), BF16), ((2 * chans, 2 * mid), BF16)
    single, double = ((3 * mid, 3 * mid), BF16), ((6 * mid, 4 * mid), BF16)
    bias = ((mid, 128), F32)
    made = [single, double, tall_w, wide_w, single, double, tall_w]
    params = [conv_reduce.swapaxes(1, 2), conv_spatial, conv_expand, scale_mid, shift_mid, scale_out, shift_out]

    def small(count):
        return (count, mid, cols), BF16

    def large(count):
        return (count, chans, cols), BF16

    inner, edge = rows - 2, 2
    row = ((mid, cols), BF16)
    acc_c = ((mid, chans), F32)
    acc_s = ((3 * mid, 3 * mid), F32)

    ids = lax.axis_index("space") * rows + lax.broadcasted_iota(jnp.int32, (rows, 128), 0)
    limits = jnp.where(ids < heights, widths, 0)
    strip = pltpu.with_memory_space_constraint(images[0], pltpu.HBM)
    mask, wr_0, b1_0, *held, slope1_0e, top, bottom = call(
        start, [((rows, 16, cols), BF16), wide_w, bias] + [(p.shape, p.dtype) for p in params] + [small(edge), row, row],
        [limits, strip] + [pltpu.with_memory_space_constraint(p, pltpu.HBM) for p in params],
        "start", [VMEM] + [HBM] * 8, scratch=[pltpu.VMEM(*large(edge)), pltpu.SemaphoreType.DMA((2 + len(params),))])
    f0a, f0b = exchange(top, bottom)
    hw = [mask]
    first0, slope1_0i, second0i, slope2_0i, slope3_0i, x1i, slope1_1i, first1i, *weights = call(
        forward_inner, [small(rows)] + [small(inner)] * 3 + [large(inner)] * 2 + [small(inner)] * 2
        + [wide_w] + [((2,) + s, d) for s, d in made] + [bias] + [((2,) + s, d) for s, d in (bias, ((chans, 128), F32))],
        hw + [images[0], top, bottom, wr_0, b1_0] + held, "forward_inner")
    wr, kf, kf2, we, we_back, kb, kb2, wr_back, b1, b2, b3 = weights
    second0e, slope2_0e, slope3_0e, x1e, slope1_1e, first1, top, bottom = call(
        forward_edge, [small(edge)] * 2 + [large(edge)] * 2 + [small(edge), small(rows), row, row],
        hw + [images[0], first0, f0a, f0b, first1i, kf, kf2, b2, we, b3, wr, b1], "forward_edge")
    f1a, f1b = exchange(top, bottom)
    turn = [kf, kf2, b2, we, b3, we_back]
    gsum1i, gmid2_1i, dexp1 = call(
        turn_inner, [large(inner), small(inner), acc_c], hw + [first1, x1i, cot] + turn, "turn_inner")
    gsum1e, gmid2_1, second1e, top, bottom = call(
        turn_edge, [large(edge), small(rows), small(edge), row, row],
        hw + [first1, f1a, f1b, x1e, cot] + turn + [gmid2_1i], "turn_edge")
    g1a, g1b = exchange(top, bottom)
    back = [kb, kb2, wr_back, we_back]
    gsum0i, gmid2_0i, dred1, dspat1, dexp1 = call(
        backward_inner, [large(inner), small(inner), acc_c, acc_s, acc_c],
        hw + [gmid2_1, first1, f1a, f1b, second1e, gsum1e, dexp1, slope1_1i, x1i, gsum1i, slope3_0i, slope2_0i] + back, "backward_inner")
    gsum0e, gmid2_0, dred1, top, bottom = call(
        backward_edge, [large(edge), small(rows), acc_c, row, row],
        hw + [gmid2_1, g1a, g1b, slope1_1e, x1e, gsum1e, slope3_0e, slope2_0e] + back + [gmid2_0i, dred1], "backward_edge")
    g0a, g0b = exchange(top, bottom)
    gmid1_0i, dred0, dspat0, dexp0 = call(
        last_inner, [small(inner), acc_c, acc_s, acc_c],
        [gmid2_0, first0, f0a, f0b, slope1_0i, images[0], second0i, second0e, gsum0i, gsum0e, kb, kb2], "last_inner")
    gmid1_0e, keep, send = call(
        last_edge, [small(edge), ((4 * mid + mid // 4, chans), BF16), ((4 * mid + mid // 4, chans), BF16)],
        [gmid2_0, g0a, g0b, slope1_0e, images[0], kb, kb2, dred0, dspat0, dred1, dexp0, dexp1, dspat1],
        "last_edge", scratch=[pltpu.VMEM(*acc_c)])
    (grad,) = call(
        grad_rows, [large(rows)], [gmid1_0i, gmid1_0e, gsum0i, gsum0e, wr_back], "grad_images", out_specs=[HBM],
        scratch=[pltpu.VMEM(*large(rows)), pltpu.SemaphoreType.DMA((rows,))])
    mine, other, grad = all_sum(keep, send, grad)
    factor = 1.0 / math.sqrt(lax.axis_size("batch") * rows * lax.axis_size("space") * cols)
    g_reduce, g_spatial, g_expand = call(
        functools.partial(finish, factor),
        [((2, mid, chans), F32), (conv_spatial.shape, F32), ((2, mid, chans), F32)], [mine, other, scale_out], "finish")
    return grad[None], g_reduce.swapaxes(1, 2), g_spatial, g_expand


def solution(mesh):
    strips = P("batch", "space", None, None)
    placed = (strips, P("batch"), P("batch")) + (P(),) * 7 + (strips,)
    return jax.shard_map(
        body, mesh=mesh, in_specs=placed, out_specs=(strips, P(), P(), P()), check_vma=False)
```

```python
import functools
import math

import jax
import jax.numpy as jnp
from jax import lax
from jax.experimental import pallas as pl
from jax.experimental.pallas import tpu as pltpu
from jax.sharding import PartitionSpec as P

F32 = jnp.float32
BF16 = jnp.bfloat16
VMEM_LIMIT = 12 * 1024 * 1024
BESIDE = 1
VMEM = pl.BlockSpec(memory_space=pltpu.VMEM)
HBM = pl.BlockSpec(memory_space=pltpu.HBM)


def mm(a, b):
    return lax.dot_general(a, b, (((1,), (0,)), ((), ())), preferred_element_type=F32)


def mm_nt(a, b):
    return lax.dot_general(a, b, (((1,), (1,)), ((), ())), preferred_element_type=F32)


def gate(h):
    t = jnp.tanh(h)
    p = 1 + t
    y = h * p
    return y.astype(BF16), (p + y * (1 - t)).astype(BF16)


def wide(bias, cols):
    return jnp.concatenate([bias[...]] * (cols // bias.shape[-1]), axis=1)


def row_mask(limits, row, cols):
    limit = jnp.concatenate([limits[row : row + 1, :]] * (cols // limits.shape[1]), axis=1)
    ids = lax.broadcasted_iota(jnp.int32, (1, cols), 1)
    return jnp.where(ids < limit, 1.0, 0.0).astype(BF16)


def inside(mask, row, chans):
    return jnp.concatenate([mask[row]] * (chans // mask.shape[1]), axis=0)


def before(v):
    v = pltpu.roll(v, 1, 1)
    ids = lax.broadcasted_iota(jnp.int32, (1, 128), 1)
    edge = v[:, :128] * jnp.where(ids > 0, 1.0, 0.0).astype(v.dtype)
    return jnp.concatenate([edge, v[:, 128:]], axis=1)


def after(v):
    cols = v.shape[-1]
    v = pltpu.roll(v, cols - 1, 1)
    ids = lax.broadcasted_iota(jnp.int32, (1, 128), 1)
    edge = v[:, cols - 128 :] * jnp.where(ids < 127, 1.0, 0.0).astype(v.dtype)
    return jnp.concatenate([v[:, : cols - 128], edge], axis=1)


def edge_taps(strip, halo_above, halo_below, last):
    me = lax.axis_index("space")
    rows = strip.shape[0]
    if last:
        have = jnp.where(me < lax.axis_size("space") - 1, 1.0, 0.0).astype(BF16)
        parts = [strip[rows - 2], strip[rows - 1], halo_below[...] * have]
    else:
        have = jnp.where(me > 0, 1.0, 0.0).astype(BF16)
        parts = [halo_above[...] * have, strip[0], strip[1]]
    return jnp.concatenate(parts, axis=0)


def inner_taps(strip, row, count):
    part = strip[pl.ds(row - 1, count)]
    return part.reshape(part.shape[0] * part.shape[1], part.shape[2])


def join(out, flip):
    mid = out.shape[0] // 3
    first, centre, last = out[:mid], out[mid : 2 * mid], out[2 * mid :]
    if flip:
        first, last = last, first
    return before(first) + centre + after(last)


def spread(v):
    return jnp.concatenate([after(v), v, before(v)], axis=0)


def chunks(cols, count=1):
    return [slice(c, c + cols // count) for c in range(0, cols, cols // count)]


def reduce_part(x, w_reduce, b_first, mask):
    h = mm(w_reduce[...], x) + wide(b_first, x.shape[-1])
    y, d = gate(h)
    return y * mask, d * mask


def conv_rows(edges, rows, strip, halos, single, double, flip, work, unroll=True):
    if edges:
        ends = [mm(single[...], edge_taps(strip, *halos, last)) for last in (False, True)]
        work([(0, 0, join(ends[0], flip)), (rows - 1, 1, join(ends[1], flip))])
        return

    def pair(i, carry):
        row = 1 + 2 * i
        out = mm(double[...], inner_taps(strip, row, 4))
        half = out.shape[0] // 2
        work([(row, row - 1, join(out[:half], flip)), (row + 1, row, join(out[half:], flip))])
        return carry

    lax.fori_loop(0, (rows - 2) // 2, pair, 0, unroll=unroll)


def both(weights, pair):
    out = mm(weights, jnp.concatenate(pair, axis=0))
    half = out.shape[0] // 2
    return out[:half], out[half:]


def mm_nt_sum(pairs):
    return mm_nt(*(jnp.concatenate(side, axis=1) for side in zip(*pairs)))


def tap_terms(first, gmid2, rows):
    return mm_nt_sum([(inner_taps(first, row, 3), spread(gmid2[row])) for row in rows])


def edge_tap_terms(first, halos, gmid2):
    ends = ((False, 0), (True, first.shape[0] - 1))
    return mm_nt_sum([(edge_taps(first, *halos, last), spread(gmid2[row])) for last, row in ends])


def start_sums(have, sums):
    for value, out in zip(have or [None] * len(sums), sums):
        out[...] = jnp.zeros_like(out) if value is None else value[...]


def gather_rows(full, inner, top, bottom):
    rows = full.shape[0]
    full[0] = top[...]
    full[rows - 1] = bottom[...]
    for r in range(1, rows - 1):
        full[r] = inner[r - 1]


def forward_rows(edges, mask, rows, strip, halos, x, kf, kf2, b_second, we, b_out, w_reduce, b_first,
                 second, slope2, slope3, x1, slope1, put_first):
    cols = x.shape[-1]

    def work(pair):
        seconds = []
        for _, slot, pre in pair:
            y, d = gate(pre + wide(b_second, cols))
            second[slot] = y
            slope2[slot] = d
            seconds.append(y)
        for (row, slot, _), expanded in zip(pair, both(we[...], seconds)):
            y, d = gate(expanded + wide(b_out, cols) + x[row].astype(F32) * 0.5)
            slope3[slot] = d
            x1[slot] = y
            first, slope1[slot] = reduce_part(y, w_reduce, b_first, inside(mask, row, slope1.shape[1]))
            put_first(row, slot, first)

    conv_rows(edges, rows, strip, halos, kf, kf2, False, work)


def forward_inner(mask, x, top, bottom, wr_0, b1_0, red, spa, exp, scale_mid, shift_mid, scale_out, shift_out,
                  first0, slope1_0, second, slope2, slope3, x1, slope1_1, first1,
                  wr, kf, kf2, we, we_back, kb, kb2, wr_back, b1, b2, b3):
    rows, cols = x.shape[0], x.shape[-1]
    prepare(red, spa, exp, scale_mid, shift_mid, scale_out, shift_out, wr, kf, kf2, we, we_back, kb, kb2, wr_back, b1, b2, b3)
    first0[0] = top[...]
    first0[rows - 1] = bottom[...]

    @pl.loop(1, rows - 1, unroll=True)
    def _(row):
        first0[row], slope1_0[row - 1] = reduce_part(x[row], wr_0, b1_0, inside(mask, row, first0.shape[1]))

    def put_first(row, slot, value):
        first1[slot] = value

    forward_rows(False, mask, rows, first0, None, x, kf.at[0], kf2.at[0], b2.at[0], we.at[0], b3.at[0],
                 wr, b1, second, slope2, slope3, x1, slope1_1, put_first)


def forward_edge(mask, x, first0, above, below, first1_inner, kf, kf2, b2, we, b3, wr, b1,
                 second, slope2, slope3, x1, slope1_1, first1, top, bottom):
    def put_first(row, slot, value):
        (bottom if slot else top)[...] = value

    forward_rows(True, mask, first0.shape[0], first0, (above, below), x, kf.at[0], kf2.at[0], b2.at[0], we.at[0],
                 b3.at[0], wr, b1, second, slope2, slope3, x1, slope1_1, put_first)
    gather_rows(first1, first1_inner, top, bottom)


def turn_rows(edges, mask, first1, halos, x1, cot, kf, kf2, b2, we, b3, we_back, gsum, dexp, put_mid2, second=None):
    rows, cols = cot.shape[0], cot.shape[-1]

    def work(pair):
        gates = [gate(pre + wide(b2.at[1], cols)) for _, _, pre in pair]
        expanded = both(we[1], [y2 for y2, _ in gates])
        terms = []
        for (row, slot, _), (y2, d2), pre3 in zip(pair, gates, expanded):
            _, d3 = gate(pre3 + wide(b3.at[1], cols) + x1[slot].astype(F32) * 0.5)
            g = cot[row] * inside(mask, row, cot.shape[1]) * d3
            gsum[slot] = g
            put_mid2(row, slot, mm(we_back[1], g).astype(BF16) * d2)
            terms.append((y2, g))
            if edges:
                second[slot] = y2
        if not edges:
            dexp[...] += mm_nt_sum(terms)

    conv_rows(edges, rows, first1, halos, kf.at[1], kf2.at[1], False, work)


def turn_inner(mask, first1, x1, cot, kf, kf2, b2, we, b3, we_back, gsum, gmid2, dexp):
    start_sums(None, [dexp])

    def put_mid2(row, slot, value):
        gmid2[slot] = value

    turn_rows(False, mask, first1, None, x1, cot, kf, kf2, b2, we, b3, we_back, gsum, dexp, put_mid2)


def turn_edge(mask, first1, above, below, x1, cot, kf, kf2, b2, we, b3, we_back, gmid2_inner,
              gsum, gmid2, second, top, bottom):

    def put_mid2(row, slot, value):
        (bottom if slot else top)[...] = value

    turn_rows(True, mask, first1, (above, below), x1, cot, kf, kf2, b2, we, b3, we_back, gsum, None, put_mid2, second)
    gather_rows(gmid2, gmid2_inner, top, bottom)


def backward_rows(edges, mask, gmid2, g_halos, first1, slope1, x1, gsum1, slope3, slope2,
                  kb, kb2, wr_back, we_back, gsum0, dred, dspat, put_mid2):
    rows, cols = gmid2.shape[0], gmid2.shape[-1]

    def work(pair):
        firsts = [back.astype(BF16) * slope1[slot] for _, slot, back in pair]
        dred[...] += mm_nt_sum([(g1, x1[slot]) for g1, (_, slot, _) in zip(firsts, pair)])
        if not edges:
            dspat[...] += tap_terms(first1, gmid2, [row for row, _, _ in pair])
        ups = both(wr_back[1], firsts)
        for (row, slot, _), g1, up in zip(pair, firsts, ups):
            g = (up + gsum1[slot].astype(F32)).astype(BF16) * slope3[slot] * inside(mask, row, slope3.shape[1])
            gsum0[slot] = g
            put_mid2(row, slot, mm(we_back[0], g).astype(BF16) * slope2[slot])

    conv_rows(edges, rows, gmid2, g_halos, kb.at[1], kb2.at[1], True, work)


def backward_inner(mask, gmid2, first1, f_above, f_below, second_edge, gsum_edge, dexp_turn, slope1, x1, gsum1, slope3, slope2, kb, kb2, wr_back, we_back,
                   gsum0, gmid2_0, dred, dspat, dexp):
    start_sums(None, [dred])
    dspat[...] = edge_tap_terms(first1, (f_above, f_below), gmid2)
    dexp[...] = dexp_turn[...] + mm_nt_sum([(second_edge[n], gsum_edge[n]) for n in range(2)])

    def put_mid2(row, slot, value):
        gmid2_0[slot] = value

    backward_rows(False, mask, gmid2, None, first1, slope1, x1, gsum1, slope3, slope2,
                  kb, kb2, wr_back, we_back, gsum0, dred, dspat, put_mid2)


def backward_edge(mask, gmid2, above, below, slope1, x1, gsum1, slope3, slope2,
                  kb, kb2, wr_back, we_back, gmid2_inner, dred_inner,
                  gsum0, gmid2_0, dred, top, bottom):
    start_sums([dred_inner], [dred])

    def put_mid2(row, slot, value):
        (bottom if slot else top)[...] = value

    backward_rows(True, mask, gmid2, (above, below), None, slope1, x1, gsum1, slope3,
                  slope2, kb, kb2, wr_back, we_back, gsum0, dred, None, put_mid2)
    gather_rows(gmid2_0, gmid2_inner, top, bottom)


def last_rows(edges, gmid2, g_halos, first0, slope1, x, kb, kb2, gmid1, dred, dspat):
    def work(pair):
        firsts = []
        for row, slot, back in pair:
            g1 = back.astype(BF16) * slope1[slot]
            gmid1[slot] = g1
            firsts.append((g1, x[row]))
        dred[...] += mm_nt_sum(firsts)
        if not edges:
            dspat[...] += tap_terms(first0, gmid2, [row for row, _, _ in pair])

    conv_rows(edges, gmid2.shape[0], gmid2, g_halos, kb.at[0], kb2.at[0], True, work, False)


def last_inner(gmid2, first0, f_above, f_below, slope1, x, second_inner, second_edge, gsum_inner, gsum_edge, kb, kb2,
               gmid1, dred, dspat, dexp):
    start_sums(None, [dred])
    dspat[...] = edge_tap_terms(first0, (f_above, f_below), gmid2)
    dexp[...] = mm_nt(second_edge[0], gsum_edge[0]) + mm_nt(second_edge[1], gsum_edge[1])

    @pl.loop(0, second_inner.shape[0] // 2)
    def _(i):
        dexp[...] += mm_nt_sum([(second_inner[2 * i], gsum_inner[2 * i]), (second_inner[2 * i + 1], gsum_inner[2 * i + 1])])

    last_rows(False, gmid2, None, first0, slope1, x, kb, kb2, gmid1, dred, dspat)


def tap_places(mid):
    places = []
    for n in range(9):
        a, b = divmod(n, 3)
        if n < 8:
            base, at = (2 + n // 4) * mid, n % 4
            places.append((slice(a * mid, (a + 1) * mid), slice(b * mid, (b + 1) * mid),
                           slice(base, base + mid), slice(at * mid, (at + 1) * mid)))
        else:
            part = mid // 4
            for q in range(4):
                places.append((slice(a * mid + q * part, a * mid + (q + 1) * part), slice(b * mid, (b + 1) * mid),
                               slice(4 * mid, 4 * mid + part), slice(q * mid, (q + 1) * mid)))
    return places


def last_edge(gmid2, above, below, slope1, x, kb, kb2, dred_inner, dspat,
              dred1, dexp0, dexp1, dspat1, gmid1, keep, send, dred):
    start_sums([dred_inner], [dred])
    last_rows(True, gmid2, (above, below), None, slope1, x, kb, kb2, gmid1, dred, None)
    core = lax.axis_index("batch") % 2

    def pack(out, reduce_term, expand_term, spatial_term):
        mid = reduce_term.shape[0]
        out[:mid] = reduce_term[...].astype(BF16)
        out[mid : 2 * mid] = expand_term[...].astype(BF16)
        for rows_in, cols_in, rows_out, cols_out in tap_places(mid):
            out[rows_out, cols_out] = spatial_term[rows_in, cols_in].astype(BF16)

    for own in range(2):
        @pl.when(core == own)
        def _():
            blocks = ((dred, dexp0, dspat), (dred1, dexp1, dspat1))
            pack(keep, *blocks[own])
            pack(send, *blocks[1 - own])


def grad_rows(gmid1_inner, gmid1_edge, gsum_inner, gsum_edge, wr_back, out, held, sems):
    rows = held.shape[0]

    def work(at, slots, gmid1, gsum):
        for row, slot, acc in zip(at, slots, both(wr_back[0], [gmid1[slot] for slot in slots])):
            held[row] = (acc + gsum[slot].astype(F32) * 0.25).astype(BF16)
            pltpu.make_async_copy(held.at[row], out.at[row], sems.at[row]).start()

    @pl.loop(0, (rows - 2) // 2, unroll=True)
    def _(i):
        work((2 * i + 1, 2 * i + 2), (2 * i, 2 * i + 1), gmid1_inner, gsum_inner)

    work((0, rows - 1), (0, 1), gmid1_edge, gsum_edge)
    for r in range(rows):
        pltpu.make_async_copy(held.at[r], out.at[r], sems.at[r]).wait()


def finish(factor, mine, other, scale_out, g_reduce, g_spatial, g_expand):
    mid = g_reduce.shape[1]
    core = lax.axis_index("batch") % 2
    for terms, k in ((mine, core), (other, 1 - core)):
        g_reduce[k] = terms[:mid].astype(F32) * factor
        scale = jnp.where(k == 0, scale_out[0:1, :] * (factor * 0.25), scale_out[1:2, :] * (factor * 0.5))
        g_expand[k] = terms[mid : 2 * mid].astype(F32) * scale
        for rows_in, cols_in, rows_out, cols_out in tap_places(mid):
            a, b = rows_in.start // mid, cols_in.start // mid
            part = terms[rows_out, cols_out].astype(F32) * factor
            g_spatial[k, a, b, rows_in.start - a * mid : rows_in.stop - a * mid] = part


def lanes(vector, count):
    return jnp.broadcast_to(vector, (count, vector.shape[-1])).T


def twin(out, k, value):
    tall, across = value.shape
    out[k, :tall, :across] = value
    out[k, tall:, across:] = value


def start(limits, images, red_h, spa_h, exp_h, sm_h, sh_h, so_h, sho_h,
          mask, wr, b1, red, spa, exp, scale_mid, shift_mid, scale_out, shift_out, slope1, top, bottom, x, sems):
    rows, cols = images.shape[0], x.shape[-1]
    copies = [pltpu.make_async_copy(s, d, sems.at[n]) for n, (s, d) in enumerate(
        ((sm_h, scale_mid), (sh_h, shift_mid), (red_h, red), (images.at[0], x.at[0]), (images.at[rows - 1], x.at[1]),
         (spa_h, spa), (exp_h, exp), (so_h, scale_out), (sho_h, shift_out)))]
    for copy in copies:
        copy.start()
    for copy in copies[:3]:
        copy.wait()
    for row in range(rows):
        mask[row] = jnp.broadcast_to(row_mask(limits, row, cols), mask.shape[1:])
    wr[...] = (red[0].astype(F32) * (0.5 * lanes(scale_mid[0, 0:1, :], red.shape[-1]))).astype(BF16)
    b1[...] = 0.5 * lanes(shift_mid[0, 0:1, :], b1.shape[-1])
    for slot, (row, edge) in enumerate(((0, top), (rows - 1, bottom))):
        copies[3 + slot].wait()
        edge[...], slope1[slot] = reduce_part(x[slot], wr, b1, inside(mask, row, edge.shape[0]))
    for copy in copies[5:]:
        copy.wait()


def prepare(red, spa, exp, scale_mid, shift_mid, scale_out, shift_out,
            wr, kf, kf2, we, we_back, kb, kb2, wr_back, b1, b2, b3):
    mid = red.shape[1]
    for out in (kf2, kb2, we, wr_back):
        out[...] = jnp.zeros_like(out)
    for k in range(2):
        twice = 2.0 ** (2 - k)
        s1, s2 = scale_mid[k, 0:1, :], scale_mid[k, 1:2, :]
        so = scale_out[k : k + 1, :]
        r, e = red[k].astype(F32), exp[k].astype(F32)
        chans = r.shape[-1]
        if k == 1:
            wr[...] = (r * (0.5 * lanes(s1, chans))).astype(BF16)
            b1[...] = 0.5 * lanes(shift_mid[k, 0:1, :], b1.shape[-1])
        twin(wr_back, k, (r * (1.0 if k == 0 else twice)).T.astype(BF16))
        twin(we, k, (e * (0.5 * so)).T.astype(BF16))
        we_back[k] = (e * (so * (0.5 / twice)) * lanes(s2, chans)).astype(BF16)
        half = 0.5 * lanes(s1, mid)
        for a in range(3):
            for b in range(3):
                part = spa[k, a, b].astype(F32)
                ahead = (part * (0.5 * s2)).T.astype(BF16)
                back = (part * half).astype(BF16)
                for out, out2, value, at in ((kf, kf2, ahead, a), (kb, kb2, back, 2 - a)):
                    out[k, b * mid : (b + 1) * mid, at * mid : (at + 1) * mid] = value
                    for j in range(2):
                        out2[k, (3 * j + b) * mid : (3 * j + b + 1) * mid, (at + j) * mid : (at + j + 1) * mid] = value
        b2[k] = 0.5 * lanes(shift_mid[k, 1:2, :], b2.shape[-1])
        b3[k] = 0.5 * lanes(shift_out[k : k + 1, :], b3.shape[-1])


def call(kernel, outs, args, name, specs=None, out_specs=None, scratch=(), limit=VMEM_LIMIT):
    return pl.pallas_call(
        kernel,
        in_specs=specs or [VMEM] * len(args),
        out_specs=out_specs or [VMEM] * len(outs),
        out_shape=[jax.ShapeDtypeStruct(s, d) for s, d in outs],
        scratch_shapes=list(scratch),
        compiler_params=pltpu.CompilerParams(vmem_limit_bytes=limit),
        name=name,
    )(*args)


def exchange(top, bottom):
    count = lax.axis_size("space")
    above = lax.ppermute(bottom, "space", [(i, (i + 1) % count) for i in range(count)])
    below = lax.ppermute(top, "space", [((i + 1) % count, i) for i in range(count)])
    return above, below


def swaps():
    def flat(z, x, core, y):
        return ((z % 2 * 4 + x) * 2 + core) * 8 + y * 2 + z // 2

    places = [(z, x, core, y) for z in range(4) for x in range(4) for core in range(2) for y in range(4)]
    orders = ((1, 3, 0), (3, 0, 1))
    steps = []
    for turn in range(3):
        steps.append([[(flat(*at), flat(*(c ^ mirror if n == orders[at[2]][turn] else c for n, c in enumerate(at))))
                       for at in places] for mirror in (2, 1, 3)])
    return steps


def all_sum(keep, send, beside):
    cores = [(i, i ^ 1) for i in range(lax.axis_size("batch"))]
    value = keep.astype(F32) + lax.ppermute(send, "batch", cores).astype(F32)
    for step, ring in enumerate(swaps()):
        if step == BESIDE:
            value, beside = lax.optimization_barrier((value, beside))
        rounded = value.astype(BF16)
        for got in [lax.ppermute(rounded, ("batch", "space"), pairs) for pairs in ring]:
            value = value + got.astype(F32)
    mine = value.astype(BF16)
    return mine, lax.ppermute(mine, "batch", cores), beside


def body(images, heights, widths, conv_reduce, conv_spatial, conv_expand, scale_mid, shift_mid,
         scale_out, shift_out, cotangent):
    _, rows, chans, cols = images.shape
    mid = conv_reduce.shape[-1]
    cot = cotangent[0]
    wide_w, tall_w = ((mid, chans), BF16), ((2 * chans, 2 * mid), BF16)
    single, double = ((3 * mid, 3 * mid), BF16), ((6 * mid, 4 * mid), BF16)
    bias = ((mid, 128), F32)
    made = [single, double, tall_w, wide_w, single, double, tall_w]
    params = [conv_reduce.swapaxes(1, 2), conv_spatial, conv_expand, scale_mid, shift_mid, scale_out, shift_out]

    def small(count):
        return (count, mid, cols), BF16

    def large(count):
        return (count, chans, cols), BF16

    inner, edge = rows - 2, 2
    row = ((mid, cols), BF16)
    acc_c = ((mid, chans), F32)
    acc_s = ((3 * mid, 3 * mid), F32)

    ids = lax.axis_index("space") * rows + lax.broadcasted_iota(jnp.int32, (rows, 128), 0)
    limits = jnp.where(ids < heights, widths, 0)
    strip = pltpu.with_memory_space_constraint(images[0], pltpu.HBM)
    mask, wr_0, b1_0, *held, slope1_0e, top, bottom = call(
        start, [((rows, 16, cols), BF16), wide_w, bias] + [(p.shape, p.dtype) for p in params] + [small(edge), row, row],
        [limits, strip] + [pltpu.with_memory_space_constraint(p, pltpu.HBM) for p in params],
        "start", [VMEM] + [HBM] * 8, scratch=[pltpu.VMEM(*large(edge)), pltpu.SemaphoreType.DMA((2 + len(params),))])
    f0a, f0b = exchange(top, bottom)
    hw = [mask]
    first0, slope1_0i, second0i, slope2_0i, slope3_0i, x1i, slope1_1i, first1i, *weights = call(
        forward_inner, [small(rows)] + [small(inner)] * 3 + [large(inner)] * 2 + [small(inner)] * 2
        + [wide_w] + [((2,) + s, d) for s, d in made] + [bias] + [((2,) + s, d) for s, d in (bias, ((chans, 128), F32))],
        hw + [images[0], top, bottom, wr_0, b1_0] + held, "forward_inner")
    wr, kf, kf2, we, we_back, kb, kb2, wr_back, b1, b2, b3 = weights
    second0e, slope2_0e, slope3_0e, x1e, slope1_1e, first1, top, bottom = call(
        forward_edge, [small(edge)] * 2 + [large(edge)] * 2 + [small(edge), small(rows), row, row],
        hw + [images[0], first0, f0a, f0b, first1i, kf, kf2, b2, we, b3, wr, b1], "forward_edge")
    f1a, f1b = exchange(top, bottom)
    turn = [kf, kf2, b2, we, b3, we_back]
    gsum1i, gmid2_1i, dexp1 = call(
        turn_inner, [large(inner), small(inner), acc_c], hw + [first1, x1i, cot] + turn, "turn_inner")
    gsum1e, gmid2_1, second1e, top, bottom = call(
        turn_edge, [large(edge), small(rows), small(edge), row, row],
        hw + [first1, f1a, f1b, x1e, cot] + turn + [gmid2_1i], "turn_edge")
    g1a, g1b = exchange(top, bottom)
    back = [kb, kb2, wr_back, we_back]
    gsum0i, gmid2_0i, dred1, dspat1, dexp1 = call(
        backward_inner, [large(inner), small(inner), acc_c, acc_s, acc_c],
        hw + [gmid2_1, first1, f1a, f1b, second1e, gsum1e, dexp1, slope1_1i, x1i, gsum1i, slope3_0i, slope2_0i] + back, "backward_inner")
    gsum0e, gmid2_0, dred1, top, bottom = call(
        backward_edge, [large(edge), small(rows), acc_c, row, row],
        hw + [gmid2_1, g1a, g1b, slope1_1e, x1e, gsum1e, slope3_0e, slope2_0e] + back + [gmid2_0i, dred1], "backward_edge")
    g0a, g0b = exchange(top, bottom)
    gmid1_0i, dred0, dspat0, dexp0 = call(
        last_inner, [small(inner), acc_c, acc_s, acc_c],
        [gmid2_0, first0, f0a, f0b, slope1_0i, images[0], second0i, second0e, gsum0i, gsum0e, kb, kb2], "last_inner")
    gmid1_0e, keep, send = call(
        last_edge, [small(edge), ((4 * mid + mid // 4, chans), BF16), ((4 * mid + mid // 4, chans), BF16)],
        [gmid2_0, g0a, g0b, slope1_0e, images[0], kb, kb2, dred0, dspat0, dred1, dexp0, dexp1, dspat1],
        "last_edge", scratch=[pltpu.VMEM(*acc_c)])
    (grad,) = call(
        grad_rows, [large(rows)], [gmid1_0i, gmid1_0e, gsum0i, gsum0e, wr_back], "grad_images", out_specs=[HBM],
        scratch=[pltpu.VMEM(*large(rows)), pltpu.SemaphoreType.DMA((rows,))])
    mine, other, grad = all_sum(keep, send, grad)
    factor = 1.0 / math.sqrt(lax.axis_size("batch") * rows * lax.axis_size("space") * cols)
    g_reduce, g_spatial, g_expand = call(
        functools.partial(finish, factor),
        [((2, mid, chans), F32), (conv_spatial.shape, F32), ((2, mid, chans), F32)], [mine, other, scale_out], "finish")
    return grad[None], g_reduce.swapaxes(1, 2), g_spatial, g_expand


def solution(mesh):
    strips = P("batch", "space", None, None)
    placed = (strips, P("batch"), P("batch")) + (P(),) * 7 + (strips,)
    return jax.shard_map(
        body, mesh=mesh, in_specs=placed, out_specs=(strips, P(), P(), P()), check_vma=False)
```

```python
import functools
import math

import jax
import jax.numpy as jnp
from jax import lax
from jax.experimental import pallas as pl
from jax.experimental.pallas import tpu as pltpu
from jax.sharding import PartitionSpec as P

F32 = jnp.float32
BF16 = jnp.bfloat16
VMEM_LIMIT = 12 * 1024 * 1024
BESIDE = 1
VMEM = pl.BlockSpec(memory_space=pltpu.VMEM)
HBM = pl.BlockSpec(memory_space=pltpu.HBM)


def mm(a, b):
    return lax.dot_general(a, b, (((1,), (0,)), ((), ())), preferred_element_type=F32)


def mm_nt(a, b):
    return lax.dot_general(a, b, (((1,), (1,)), ((), ())), preferred_element_type=F32)


def gate(h):
    t = jnp.tanh(h)
    p = 1 + t
    y = h * p
    return y.astype(BF16), (p + y * (1 - t)).astype(BF16)


def wide(bias, cols):
    return jnp.concatenate([bias[...]] * (cols // bias.shape[-1]), axis=1)


def row_mask(limits, row, cols):
    limit = jnp.concatenate([limits[row : row + 1, :]] * (cols // limits.shape[1]), axis=1)
    ids = lax.broadcasted_iota(jnp.int32, (1, cols), 1)
    return jnp.where(ids < limit, 1.0, 0.0).astype(BF16)


def inside(mask, row, chans):
    return jnp.concatenate([mask[row]] * (chans // mask.shape[1]), axis=0)


def before(v):
    v = pltpu.roll(v, 1, 1)
    ids = lax.broadcasted_iota(jnp.int32, (1, 128), 1)
    edge = v[:, :128] * jnp.where(ids > 0, 1.0, 0.0).astype(v.dtype)
    return jnp.concatenate([edge, v[:, 128:]], axis=1)


def after(v):
    cols = v.shape[-1]
    v = pltpu.roll(v, cols - 1, 1)
    ids = lax.broadcasted_iota(jnp.int32, (1, 128), 1)
    edge = v[:, cols - 128 :] * jnp.where(ids < 127, 1.0, 0.0).astype(v.dtype)
    return jnp.concatenate([v[:, : cols - 128], edge], axis=1)


def edge_taps(strip, halo_above, halo_below, last):
    me = lax.axis_index("space")
    rows = strip.shape[0]
    if last:
        have = jnp.where(me < lax.axis_size("space") - 1, 1.0, 0.0).astype(BF16)
        parts = [strip[rows - 2], strip[rows - 1], halo_below[...] * have]
    else:
        have = jnp.where(me > 0, 1.0, 0.0).astype(BF16)
        parts = [halo_above[...] * have, strip[0], strip[1]]
    return jnp.concatenate(parts, axis=0)


def inner_taps(strip, row, count):
    part = strip[pl.ds(row - 1, count)]
    return part.reshape(part.shape[0] * part.shape[1], part.shape[2])


def join(out, flip):
    mid = out.shape[0] // 3
    first, centre, last = out[:mid], out[mid : 2 * mid], out[2 * mid :]
    if flip:
        first, last = last, first
    return before(first) + centre + after(last)


def spread(v):
    return jnp.concatenate([after(v), v, before(v)], axis=0)


def chunks(cols, count=1):
    return [slice(c, c + cols // count) for c in range(0, cols, cols // count)]


def reduce_part(x, w_reduce, b_first, mask):
    h = mm(w_reduce[...], x) + wide(b_first, x.shape[-1])
    y, d = gate(h)
    return y * mask, d * mask


def conv_rows(edges, rows, strip, halos, single, double, flip, work, unroll=True):
    if edges:
        ends = [mm(single[...], edge_taps(strip, *halos, last)) for last in (False, True)]
        work([(0, 0, join(ends[0], flip)), (rows - 1, 1, join(ends[1], flip))])
        return

    def pair(i, carry):
        row = 1 + 2 * i
        out = mm(double[...], inner_taps(strip, row, 4))
        half = out.shape[0] // 2
        work([(row, row - 1, join(out[:half], flip)), (row + 1, row, join(out[half:], flip))])
        return carry

    lax.fori_loop(0, (rows - 2) // 2, pair, 0, unroll=unroll)


def both(weights, pair):
    out = mm(weights, jnp.concatenate(pair, axis=0))
    half = out.shape[0] // 2
    return out[:half], out[half:]


def mm_nt_sum(pairs):
    return mm_nt(*(jnp.concatenate(side, axis=1) for side in zip(*pairs)))


def tap_terms(first, gmid2, rows):
    return mm_nt_sum([(inner_taps(first, row, 3), spread(gmid2[row])) for row in rows])


def edge_tap_terms(first, halos, gmid2):
    ends = ((False, 0), (True, first.shape[0] - 1))
    return mm_nt_sum([(edge_taps(first, *halos, last), spread(gmid2[row])) for last, row in ends])


def start_sums(have, sums):
    for value, out in zip(have or [None] * len(sums), sums):
        out[...] = jnp.zeros_like(out) if value is None else value[...]


def gather_rows(full, inner, top, bottom):
    rows = full.shape[0]
    full[0] = top[...]
    full[rows - 1] = bottom[...]
    for r in range(1, rows - 1):
        full[r] = inner[r - 1]


def forward_rows(edges, mask, rows, strip, halos, x, kf, kf2, b_second, we, b_out, w_reduce, b_first,
                 second, slope2, slope3, x1, slope1, put_first):
    cols = x.shape[-1]

    def work(pair):
        seconds = []
        for _, slot, pre in pair:
            y, d = gate(pre + wide(b_second, cols))
            second[slot] = y
            slope2[slot] = d
            seconds.append(y)
        for (row, slot, _), expanded in zip(pair, both(we[...], seconds)):
            y, d = gate(expanded + wide(b_out, cols) + x[row].astype(F32) * 0.5)
            slope3[slot] = d
            x1[slot] = y
            first, slope1[slot] = reduce_part(y, w_reduce, b_first, inside(mask, row, slope1.shape[1]))
            put_first(row, slot, first)

    conv_rows(edges, rows, strip, halos, kf, kf2, False, work)


def forward_inner(mask, x, top, bottom, wr_0, b1_0, red, spa, exp, scale_mid, shift_mid, scale_out, shift_out,
                  first0, slope1_0, second, slope2, slope3, x1, slope1_1, first1,
                  wr, kf, kf2, we, we_back, kb, kb2, wr_back, b1, b2, b3):
    rows, cols = x.shape[0], x.shape[-1]
    prepare(red, spa, exp, scale_mid, shift_mid, scale_out, shift_out, wr, kf, kf2, we, we_back, kb, kb2, wr_back, b1, b2, b3)
    first0[0] = top[...]
    first0[rows - 1] = bottom[...]

    @pl.loop(1, rows - 1, unroll=True)
    def _(row):
        first0[row], slope1_0[row - 1] = reduce_part(x[row], wr_0, b1_0, inside(mask, row, first0.shape[1]))

    def put_first(row, slot, value):
        first1[slot] = value

    forward_rows(False, mask, rows, first0, None, x, kf.at[0], kf2.at[0], b2.at[0], we.at[0], b3.at[0],
                 wr, b1, second, slope2, slope3, x1, slope1_1, put_first)


def forward_edge(mask, x, first0, above, below, first1_inner, kf, kf2, b2, we, b3, wr, b1,
                 second, slope2, slope3, x1, slope1_1, first1, top, bottom):
    def put_first(row, slot, value):
        (bottom if slot else top)[...] = value

    forward_rows(True, mask, first0.shape[0], first0, (above, below), x, kf.at[0], kf2.at[0], b2.at[0], we.at[0],
                 b3.at[0], wr, b1, second, slope2, slope3, x1, slope1_1, put_first)
    gather_rows(first1, first1_inner, top, bottom)


def turn_rows(edges, mask, first1, halos, x1, cot, kf, kf2, b2, we, b3, we_back, gsum, dexp, put_mid2, second=None):
    rows, cols = cot.shape[0], cot.shape[-1]

    def work(pair):
        gates = [gate(pre + wide(b2.at[1], cols)) for _, _, pre in pair]
        expanded = both(we[1], [y2 for y2, _ in gates])
        terms = []
        for (row, slot, _), (y2, d2), pre3 in zip(pair, gates, expanded):
            _, d3 = gate(pre3 + wide(b3.at[1], cols) + x1[slot].astype(F32) * 0.5)
            g = cot[row] * inside(mask, row, cot.shape[1]) * d3
            gsum[slot] = g
            put_mid2(row, slot, mm(we_back[1], g).astype(BF16) * d2)
            terms.append((y2, g))
            if edges:
                second[slot] = y2
        if not edges:
            dexp[...] += mm_nt_sum(terms)

    conv_rows(edges, rows, first1, halos, kf.at[1], kf2.at[1], False, work)


def turn_inner(mask, first1, x1, cot, kf, kf2, b2, we, b3, we_back, gsum, gmid2, dexp):
    start_sums(None, [dexp])

    def put_mid2(row, slot, value):
        gmid2[slot] = value

    turn_rows(False, mask, first1, None, x1, cot, kf, kf2, b2, we, b3, we_back, gsum, dexp, put_mid2)


def turn_edge(mask, first1, above, below, x1, cot, kf, kf2, b2, we, b3, we_back, gmid2_inner,
              gsum, gmid2, second, top, bottom):

    def put_mid2(row, slot, value):
        (bottom if slot else top)[...] = value

    turn_rows(True, mask, first1, (above, below), x1, cot, kf, kf2, b2, we, b3, we_back, gsum, None, put_mid2, second)
    gather_rows(gmid2, gmid2_inner, top, bottom)


def backward_rows(edges, mask, gmid2, g_halos, first1, slope1, x1, gsum1, slope3, slope2,
                  kb, kb2, wr_back, we_back, gsum0, dred, dspat, put_mid2):
    rows, cols = gmid2.shape[0], gmid2.shape[-1]

    def work(pair):
        firsts = [back.astype(BF16) * slope1[slot] for _, slot, back in pair]
        dred[...] += mm_nt_sum([(g1, x1[slot]) for g1, (_, slot, _) in zip(firsts, pair)])
        if not edges:
            dspat[...] += tap_terms(first1, gmid2, [row for row, _, _ in pair])
        ups = both(wr_back[1], firsts)
        for (row, slot, _), g1, up in zip(pair, firsts, ups):
            g = (up + gsum1[slot].astype(F32)).astype(BF16) * slope3[slot] * inside(mask, row, slope3.shape[1])
            gsum0[slot] = g
            put_mid2(row, slot, mm(we_back[0], g).astype(BF16) * slope2[slot])

    conv_rows(edges, rows, gmid2, g_halos, kb.at[1], kb2.at[1], True, work)


def backward_inner(mask, gmid2, first1, f_above, f_below, second_edge, gsum_edge, dexp_turn, slope1, x1, gsum1, slope3, slope2, kb, kb2, wr_back, we_back,
                   gsum0, gmid2_0, dred, dspat, dexp):
    start_sums(None, [dred])
    dspat[...] = edge_tap_terms(first1, (f_above, f_below), gmid2)
    dexp[...] = dexp_turn[...] + mm_nt_sum([(second_edge[n], gsum_edge[n]) for n in range(2)])

    def put_mid2(row, slot, value):
        gmid2_0[slot] = value

    backward_rows(False, mask, gmid2, None, first1, slope1, x1, gsum1, slope3, slope2,
                  kb, kb2, wr_back, we_back, gsum0, dred, dspat, put_mid2)


def backward_edge(mask, gmid2, above, below, slope1, x1, gsum1, slope3, slope2,
                  kb, kb2, wr_back, we_back, gmid2_inner, dred_inner,
                  gsum0, gmid2_0, dred, top, bottom):
    start_sums([dred_inner], [dred])

    def put_mid2(row, slot, value):
        (bottom if slot else top)[...] = value

    backward_rows(True, mask, gmid2, (above, below), None, slope1, x1, gsum1, slope3,
                  slope2, kb, kb2, wr_back, we_back, gsum0, dred, None, put_mid2)
    gather_rows(gmid2_0, gmid2_inner, top, bottom)


def last_rows(edges, gmid2, g_halos, first0, slope1, x, kb, kb2, gmid1, dred, dspat):
    def work(pair):
        firsts = []
        for row, slot, back in pair:
            g1 = back.astype(BF16) * slope1[slot]
            gmid1[slot] = g1
            firsts.append((g1, x[row]))
        dred[...] += mm_nt_sum(firsts)
        if not edges:
            dspat[...] += tap_terms(first0, gmid2, [row for row, _, _ in pair])

    conv_rows(edges, gmid2.shape[0], gmid2, g_halos, kb.at[0], kb2.at[0], True, work, False)


def last_inner(gmid2, first0, f_above, f_below, slope1, x, second_inner, second_edge, gsum_inner, gsum_edge, kb, kb2,
               gmid1, dred, dspat, dexp):
    start_sums(None, [dred])
    dspat[...] = edge_tap_terms(first0, (f_above, f_below), gmid2)
    dexp[...] = mm_nt(second_edge[0], gsum_edge[0]) + mm_nt(second_edge[1], gsum_edge[1])

    @pl.loop(0, second_inner.shape[0] // 2)
    def _(i):
        dexp[...] += mm_nt_sum([(second_inner[2 * i], gsum_inner[2 * i]), (second_inner[2 * i + 1], gsum_inner[2 * i + 1])])

    last_rows(False, gmid2, None, first0, slope1, x, kb, kb2, gmid1, dred, dspat)


def tap_places(mid):
    places = []
    for n in range(9):
        a, b = divmod(n, 3)
        if n < 8:
            base, at = (2 + n // 4) * mid, n % 4
            places.append((slice(a * mid, (a + 1) * mid), slice(b * mid, (b + 1) * mid),
                           slice(base, base + mid), slice(at * mid, (at + 1) * mid)))
        else:
            part = mid // 4
            for q in range(4):
                places.append((slice(a * mid + q * part, a * mid + (q + 1) * part), slice(b * mid, (b + 1) * mid),
                               slice(4 * mid, 4 * mid + part), slice(q * mid, (q + 1) * mid)))
    return places


def last_edge(gmid2, above, below, slope1, x, kb, kb2, dred_inner, dspat,
              dred1, dexp0, dexp1, dspat1, gmid1, keep, send, dred):
    start_sums([dred_inner], [dred])
    last_rows(True, gmid2, (above, below), None, slope1, x, kb, kb2, gmid1, dred, None)
    core = lax.axis_index("batch") % 2

    def pack(out, reduce_term, expand_term, spatial_term):
        mid = reduce_term.shape[0]
        out[:mid] = reduce_term[...].astype(BF16)
        out[mid : 2 * mid] = expand_term[...].astype(BF16)
        for rows_in, cols_in, rows_out, cols_out in tap_places(mid):
            out[rows_out, cols_out] = spatial_term[rows_in, cols_in].astype(BF16)

    for own in range(2):
        @pl.when(core == own)
        def _():
            blocks = ((dred, dexp0, dspat), (dred1, dexp1, dspat1))
            pack(keep, *blocks[own])
            pack(send, *blocks[1 - own])


def grad_rows(gmid1_inner, gmid1_edge, gsum_inner, gsum_edge, wr_back, out, held, sems):
    rows = held.shape[0]

    def work(at, slots, gmid1, gsum):
        for row, slot, acc in zip(at, slots, both(wr_back[0], [gmid1[slot] for slot in slots])):
            held[row] = (acc + gsum[slot].astype(F32) * 0.25).astype(BF16)
            pltpu.make_async_copy(held.at[row], out.at[row], sems.at[row]).start()

    @pl.loop(0, (rows - 2) // 2, unroll=True)
    def _(i):
        work((2 * i + 1, 2 * i + 2), (2 * i, 2 * i + 1), gmid1_inner, gsum_inner)

    work((0, rows - 1), (0, 1), gmid1_edge, gsum_edge)
    for r in range(rows):
        pltpu.make_async_copy(held.at[r], out.at[r], sems.at[r]).wait()


def finish(factor, mine, other, scale_out, g_reduce, g_spatial, g_expand):
    mid = g_reduce.shape[1]
    core = lax.axis_index("batch") % 2
    for terms, k in ((mine, core), (other, 1 - core)):
        g_reduce[k] = terms[:mid].astype(F32) * factor
        scale = jnp.where(k == 0, scale_out[0:1, :] * (factor * 0.25), scale_out[1:2, :] * (factor * 0.5))
        g_expand[k] = terms[mid : 2 * mid].astype(F32) * scale
        for rows_in, cols_in, rows_out, cols_out in tap_places(mid):
            a, b = rows_in.start // mid, cols_in.start // mid
            part = terms[rows_out, cols_out].astype(F32) * factor
            g_spatial[k, a, b, rows_in.start - a * mid : rows_in.stop - a * mid] = part


def lanes(vector, count):
    return jnp.broadcast_to(vector, (count, vector.shape[-1])).T


def twin(out, k, value):
    tall, across = value.shape
    out[k, :tall, :across] = value
    out[k, tall:, across:] = value


def start(limits, images, red_h, spa_h, exp_h, sm_h, sh_h, so_h, sho_h,
          mask, wr, b1, red, spa, exp, scale_mid, shift_mid, scale_out, shift_out, slope1, top, bottom, x, sems):
    rows, cols = images.shape[0], x.shape[-1]
    copies = [pltpu.make_async_copy(s, d, sems.at[n]) for n, (s, d) in enumerate(
        ((sm_h, scale_mid), (sh_h, shift_mid), (red_h, red), (images.at[0], x.at[0]), (images.at[rows - 1], x.at[1]),
         (spa_h, spa), (exp_h, exp), (so_h, scale_out), (sho_h, shift_out)))]
    for copy in copies:
        copy.start()
    for copy in copies[:3]:
        copy.wait()
    for row in range(rows):
        mask[row] = jnp.broadcast_to(row_mask(limits, row, cols), mask.shape[1:])
    wr[...] = (red[0].astype(F32) * (0.5 * lanes(scale_mid[0, 0:1, :], red.shape[-1]))).astype(BF16)
    b1[...] = 0.5 * lanes(shift_mid[0, 0:1, :], b1.shape[-1])
    for slot, (row, edge) in enumerate(((0, top), (rows - 1, bottom))):
        copies[3 + slot].wait()
        edge[...], slope1[slot] = reduce_part(x[slot], wr, b1, inside(mask, row, edge.shape[0]))
    for copy in copies[5:]:
        copy.wait()


def prepare(red, spa, exp, scale_mid, shift_mid, scale_out, shift_out,
            wr, kf, kf2, we, we_back, kb, kb2, wr_back, b1, b2, b3):
    mid = red.shape[1]
    for out in (kf2, kb2, we, wr_back):
        out[...] = jnp.zeros_like(out)
    for k in range(2):
        twice = 2.0 ** (2 - k)
        s1, s2 = scale_mid[k, 0:1, :], scale_mid[k, 1:2, :]
        so = scale_out[k : k + 1, :]
        r, e = red[k].astype(F32), exp[k].astype(F32)
        chans = r.shape[-1]
        if k == 1:
            wr[...] = (r * (0.5 * lanes(s1, chans))).astype(BF16)
            b1[...] = 0.5 * lanes(shift_mid[k, 0:1, :], b1.shape[-1])
        twin(wr_back, k, (r * (1.0 if k == 0 else twice)).T.astype(BF16))
        twin(we, k, (e * (0.5 * so)).T.astype(BF16))
        we_back[k] = (e * (so * (0.5 / twice)) * lanes(s2, chans)).astype(BF16)
        half = 0.5 * lanes(s1, mid)
        for a in range(3):
            for b in range(3):
                part = spa[k, a, b].astype(F32)
                ahead = (part * (0.5 * s2)).T.astype(BF16)
                back = (part * half).astype(BF16)
                for out, out2, value, at in ((kf, kf2, ahead, a), (kb, kb2, back, 2 - a)):
                    out[k, b * mid : (b + 1) * mid, at * mid : (at + 1) * mid] = value
                    for j in range(2):
                        out2[k, (3 * j + b) * mid : (3 * j + b + 1) * mid, (at + j) * mid : (at + j + 1) * mid] = value
        b2[k] = 0.5 * lanes(shift_mid[k, 1:2, :], b2.shape[-1])
        b3[k] = 0.5 * lanes(shift_out[k : k + 1, :], b3.shape[-1])


def call(kernel, outs, args, name, specs=None, out_specs=None, scratch=(), limit=VMEM_LIMIT):
    return pl.pallas_call(
        kernel,
        in_specs=specs or [VMEM] * len(args),
        out_specs=out_specs or [VMEM] * len(outs),
        out_shape=[jax.ShapeDtypeStruct(s, d) for s, d in outs],
        scratch_shapes=list(scratch),
        compiler_params=pltpu.CompilerParams(vmem_limit_bytes=limit),
        name=name,
    )(*args)


def exchange(top, bottom):
    count = lax.axis_size("space")
    above = lax.ppermute(bottom, "space", [(i, (i + 1) % count) for i in range(count)])
    below = lax.ppermute(top, "space", [((i + 1) % count, i) for i in range(count)])
    return above, below


def swaps():
    def flat(z, x, core, y):
        return ((z % 2 * 4 + x) * 2 + core) * 8 + y * 2 + z // 2

    places = [(z, x, core, y) for z in range(4) for x in range(4) for core in range(2) for y in range(4)]
    orders = ((1, 3, 0), (3, 0, 1))
    steps = []
    for turn in range(3):
        steps.append([[(flat(*at), flat(*(c ^ mirror if n == orders[at[2]][turn] else c for n, c in enumerate(at))))
                       for at in places] for mirror in (1, 3, 2)])
    return steps


def all_sum(keep, send, beside):
    cores = [(i, i ^ 1) for i in range(lax.axis_size("batch"))]
    value = keep.astype(F32) + lax.ppermute(send, "batch", cores).astype(F32)
    for step, ring in enumerate(swaps()):
        if step == BESIDE:
            value, beside = lax.optimization_barrier((value, beside))
        rounded = value.astype(BF16)
        for got in [lax.ppermute(rounded, ("batch", "space"), pairs) for pairs in ring]:
            value = value + got.astype(F32)
    mine = value.astype(BF16)
    return mine, lax.ppermute(mine, "batch", cores), beside


def body(images, heights, widths, conv_reduce, conv_spatial, conv_expand, scale_mid, shift_mid,
         scale_out, shift_out, cotangent):
    _, rows, chans, cols = images.shape
    mid = conv_reduce.shape[-1]
    cot = cotangent[0]
    wide_w, tall_w = ((mid, chans), BF16), ((2 * chans, 2 * mid), BF16)
    single, double = ((3 * mid, 3 * mid), BF16), ((6 * mid, 4 * mid), BF16)
    bias = ((mid, 128), F32)
    made = [single, double, tall_w, wide_w, single, double, tall_w]
    params = [conv_reduce.swapaxes(1, 2), conv_spatial, conv_expand, scale_mid, shift_mid, scale_out, shift_out]

    def small(count):
        return (count, mid, cols), BF16

    def large(count):
        return (count, chans, cols), BF16

    inner, edge = rows - 2, 2
    row = ((mid, cols), BF16)
    acc_c = ((mid, chans), F32)
    acc_s = ((3 * mid, 3 * mid), F32)

    ids = lax.axis_index("space") * rows + lax.broadcasted_iota(jnp.int32, (rows, 128), 0)
    limits = jnp.where(ids < heights, widths, 0)
    strip = pltpu.with_memory_space_constraint(images[0], pltpu.HBM)
    mask, wr_0, b1_0, *held, slope1_0e, top, bottom = call(
        start, [((rows, 16, cols), BF16), wide_w, bias] + [(p.shape, p.dtype) for p in params] + [small(edge), row, row],
        [limits, strip] + [pltpu.with_memory_space_constraint(p, pltpu.HBM) for p in params],
        "start", [VMEM] + [HBM] * 8, scratch=[pltpu.VMEM(*large(edge)), pltpu.SemaphoreType.DMA((2 + len(params),))])
    f0a, f0b = exchange(top, bottom)
    hw = [mask]
    first0, slope1_0i, second0i, slope2_0i, slope3_0i, x1i, slope1_1i, first1i, *weights = call(
        forward_inner, [small(rows)] + [small(inner)] * 3 + [large(inner)] * 2 + [small(inner)] * 2
        + [wide_w] + [((2,) + s, d) for s, d in made] + [bias] + [((2,) + s, d) for s, d in (bias, ((chans, 128), F32))],
        hw + [images[0], top, bottom, wr_0, b1_0] + held, "forward_inner")
    wr, kf, kf2, we, we_back, kb, kb2, wr_back, b1, b2, b3 = weights
    second0e, slope2_0e, slope3_0e, x1e, slope1_1e, first1, top, bottom = call(
        forward_edge, [small(edge)] * 2 + [large(edge)] * 2 + [small(edge), small(rows), row, row],
        hw + [images[0], first0, f0a, f0b, first1i, kf, kf2, b2, we, b3, wr, b1], "forward_edge")
    f1a, f1b = exchange(top, bottom)
    turn = [kf, kf2, b2, we, b3, we_back]
    gsum1i, gmid2_1i, dexp1 = call(
        turn_inner, [large(inner), small(inner), acc_c], hw + [first1, x1i, cot] + turn, "turn_inner")
    gsum1e, gmid2_1, second1e, top, bottom = call(
        turn_edge, [large(edge), small(rows), small(edge), row, row],
        hw + [first1, f1a, f1b, x1e, cot] + turn + [gmid2_1i], "turn_edge")
    g1a, g1b = exchange(top, bottom)
    back = [kb, kb2, wr_back, we_back]
    gsum0i, gmid2_0i, dred1, dspat1, dexp1 = call(
        backward_inner, [large(inner), small(inner), acc_c, acc_s, acc_c],
        hw + [gmid2_1, first1, f1a, f1b, second1e, gsum1e, dexp1, slope1_1i, x1i, gsum1i, slope3_0i, slope2_0i] + back, "backward_inner")
    gsum0e, gmid2_0, dred1, top, bottom = call(
        backward_edge, [large(edge), small(rows), acc_c, row, row],
        hw + [gmid2_1, g1a, g1b, slope1_1e, x1e, gsum1e, slope3_0e, slope2_0e] + back + [gmid2_0i, dred1], "backward_edge")
    g0a, g0b = exchange(top, bottom)
    gmid1_0i, dred0, dspat0, dexp0 = call(
        last_inner, [small(inner), acc_c, acc_s, acc_c],
        [gmid2_0, first0, f0a, f0b, slope1_0i, images[0], second0i, second0e, gsum0i, gsum0e, kb, kb2], "last_inner")
    gmid1_0e, keep, send = call(
        last_edge, [small(edge), ((4 * mid + mid // 4, chans), BF16), ((4 * mid + mid // 4, chans), BF16)],
        [gmid2_0, g0a, g0b, slope1_0e, images[0], kb, kb2, dred0, dspat0, dred1, dexp0, dexp1, dspat1],
        "last_edge", scratch=[pltpu.VMEM(*acc_c)])
    (grad,) = call(
        grad_rows, [large(rows)], [gmid1_0i, gmid1_0e, gsum0i, gsum0e, wr_back], "grad_images", out_specs=[HBM],
        scratch=[pltpu.VMEM(*large(rows)), pltpu.SemaphoreType.DMA((rows,))])
    mine, other, grad = all_sum(keep, send, grad)
    factor = 1.0 / math.sqrt(lax.axis_size("batch") * rows * lax.axis_size("space") * cols)
    g_reduce, g_spatial, g_expand = call(
        functools.partial(finish, factor),
        [((2, mid, chans), F32), (conv_spatial.shape, F32), ((2, mid, chans), F32)], [mine, other, scale_out], "finish")
    return grad[None], g_reduce.swapaxes(1, 2), g_spatial, g_expand


def solution(mesh):
    strips = P("batch", "space", None, None)
    placed = (strips, P("batch"), P("batch")) + (P(),) * 7 + (strips,)
    return jax.shard_map(
        body, mesh=mesh, in_specs=placed, out_specs=(strips, P(), P(), P()), check_vma=False)
```

```python
import functools
import math

import jax
import jax.numpy as jnp
from jax import lax
from jax.experimental import pallas as pl
from jax.experimental.pallas import tpu as pltpu
from jax.sharding import PartitionSpec as P

F32 = jnp.float32
BF16 = jnp.bfloat16
VMEM_LIMIT = 12 * 1024 * 1024
BESIDE = 1
VMEM = pl.BlockSpec(memory_space=pltpu.VMEM)
HBM = pl.BlockSpec(memory_space=pltpu.HBM)


def mm(a, b):
    return lax.dot_general(a, b, (((1,), (0,)), ((), ())), preferred_element_type=F32)


def mm_nt(a, b):
    return lax.dot_general(a, b, (((1,), (1,)), ((), ())), preferred_element_type=F32)


def gate(h):
    t = jnp.tanh(h)
    p = 1 + t
    y = h * p
    return y.astype(BF16), (p + y * (1 - t)).astype(BF16)


def wide(bias, cols):
    return jnp.concatenate([bias[...]] * (cols // bias.shape[-1]), axis=1)


def row_mask(limits, row, cols):
    limit = jnp.concatenate([limits[row : row + 1, :]] * (cols // limits.shape[1]), axis=1)
    ids = lax.broadcasted_iota(jnp.int32, (1, cols), 1)
    return jnp.where(ids < limit, 1.0, 0.0).astype(BF16)


def inside(mask, row, chans):
    return jnp.concatenate([mask[row]] * (chans // mask.shape[1]), axis=0)


def before(v):
    v = pltpu.roll(v, 1, 1)
    ids = lax.broadcasted_iota(jnp.int32, (1, 128), 1)
    edge = v[:, :128] * jnp.where(ids > 0, 1.0, 0.0).astype(v.dtype)
    return jnp.concatenate([edge, v[:, 128:]], axis=1)


def after(v):
    cols = v.shape[-1]
    v = pltpu.roll(v, cols - 1, 1)
    ids = lax.broadcasted_iota(jnp.int32, (1, 128), 1)
    edge = v[:, cols - 128 :] * jnp.where(ids < 127, 1.0, 0.0).astype(v.dtype)
    return jnp.concatenate([v[:, : cols - 128], edge], axis=1)


def edge_taps(strip, halo_above, halo_below, last):
    me = lax.axis_index("space")
    rows = strip.shape[0]
    if last:
        have = jnp.where(me < lax.axis_size("space") - 1, 1.0, 0.0).astype(BF16)
        parts = [strip[rows - 2], strip[rows - 1], halo_below[...] * have]
    else:
        have = jnp.where(me > 0, 1.0, 0.0).astype(BF16)
        parts = [halo_above[...] * have, strip[0], strip[1]]
    return jnp.concatenate(parts, axis=0)


def inner_taps(strip, row, count):
    part = strip[pl.ds(row - 1, count)]
    return part.reshape(part.shape[0] * part.shape[1], part.shape[2])


def join(out, flip):
    mid = out.shape[0] // 3
    first, centre, last = out[:mid], out[mid : 2 * mid], out[2 * mid :]
    if flip:
        first, last = last, first
    return before(first) + centre + after(last)


def spread(v):
    return jnp.concatenate([after(v), v, before(v)], axis=0)


def chunks(cols, count=1):
    return [slice(c, c + cols // count) for c in range(0, cols, cols // count)]


def reduce_part(x, w_reduce, b_first, mask):
    h = mm(w_reduce[...], x) + wide(b_first, x.shape[-1])
    y, d = gate(h)
    return y * mask, d * mask


def conv_rows(edges, rows, strip, halos, single, double, flip, work, unroll=True):
    if edges:
        ends = [mm(single[...], edge_taps(strip, *halos, last)) for last in (False, True)]
        work([(0, 0, join(ends[0], flip)), (rows - 1, 1, join(ends[1], flip))])
        return

    def pair(i, carry):
        row = 1 + 2 * i
        out = mm(double[...], inner_taps(strip, row, 4))
        half = out.shape[0] // 2
        work([(row, row - 1, join(out[:half], flip)), (row + 1, row, join(out[half:], flip))])
        return carry

    lax.fori_loop(0, (rows - 2) // 2, pair, 0, unroll=unroll)


def both(weights, pair):
    out = mm(weights, jnp.concatenate(pair, axis=0))
    half = out.shape[0] // 2
    return out[:half], out[half:]


def mm_nt_sum(pairs):
    return mm_nt(*(jnp.concatenate(side, axis=1) for side in zip(*pairs)))


def tap_terms(first, gmid2, rows):
    return mm_nt_sum([(inner_taps(first, row, 3), spread(gmid2[row])) for row in rows])


def edge_tap_terms(first, halos, gmid2):
    ends = ((False, 0), (True, first.shape[0] - 1))
    return mm_nt_sum([(edge_taps(first, *halos, last), spread(gmid2[row])) for last, row in ends])


def start_sums(have, sums):
    for value, out in zip(have or [None] * len(sums), sums):
        out[...] = jnp.zeros_like(out) if value is None else value[...]


def gather_rows(full, inner, top, bottom):
    rows = full.shape[0]
    full[0] = top[...]
    full[rows - 1] = bottom[...]
    for r in range(1, rows - 1):
        full[r] = inner[r - 1]


def forward_rows(edges, mask, rows, strip, halos, x, kf, kf2, b_second, we, b_out, w_reduce, b_first,
                 second, slope2, slope3, x1, slope1, put_first):
    cols = x.shape[-1]

    def work(pair):
        seconds = []
        for _, slot, pre in pair:
            y, d = gate(pre + wide(b_second, cols))
            second[slot] = y
            slope2[slot] = d
            seconds.append(y)
        for (row, slot, _), expanded in zip(pair, both(we[...], seconds)):
            y, d = gate(expanded + wide(b_out, cols) + x[row].astype(F32) * 0.5)
            slope3[slot] = d
            x1[slot] = y
            first, slope1[slot] = reduce_part(y, w_reduce, b_first, inside(mask, row, slope1.shape[1]))
            put_first(row, slot, first)

    conv_rows(edges, rows, strip, halos, kf, kf2, False, work)


def forward_inner(mask, x, top, bottom, wr_0, b1_0, red, spa, exp, scale_mid, shift_mid, scale_out, shift_out,
                  first0, slope1_0, second, slope2, slope3, x1, slope1_1, first1,
                  wr, kf, kf2, we, we_back, kb, kb2, wr_back, b1, b2, b3):
    rows, cols = x.shape[0], x.shape[-1]
    prepare(red, spa, exp, scale_mid, shift_mid, scale_out, shift_out, wr, kf, kf2, we, we_back, kb, kb2, wr_back, b1, b2, b3)
    first0[0] = top[...]
    first0[rows - 1] = bottom[...]

    @pl.loop(1, rows - 1, unroll=True)
    def _(row):
        first0[row], slope1_0[row - 1] = reduce_part(x[row], wr_0, b1_0, inside(mask, row, first0.shape[1]))

    def put_first(row, slot, value):
        first1[slot] = value

    forward_rows(False, mask, rows, first0, None, x, kf.at[0], kf2.at[0], b2.at[0], we.at[0], b3.at[0],
                 wr, b1, second, slope2, slope3, x1, slope1_1, put_first)


def forward_edge(mask, x, first0, above, below, first1_inner, kf, kf2, b2, we, b3, wr, b1,
                 second, slope2, slope3, x1, slope1_1, first1, top, bottom):
    def put_first(row, slot, value):
        (bottom if slot else top)[...] = value

    forward_rows(True, mask, first0.shape[0], first0, (above, below), x, kf.at[0], kf2.at[0], b2.at[0], we.at[0],
                 b3.at[0], wr, b1, second, slope2, slope3, x1, slope1_1, put_first)
    gather_rows(first1, first1_inner, top, bottom)


def turn_rows(edges, mask, first1, halos, x1, cot, kf, kf2, b2, we, b3, we_back, gsum, dexp, put_mid2, second=None):
    rows, cols = cot.shape[0], cot.shape[-1]

    def work(pair):
        gates = [gate(pre + wide(b2.at[1], cols)) for _, _, pre in pair]
        expanded = both(we[1], [y2 for y2, _ in gates])
        terms = []
        for (row, slot, _), (y2, d2), pre3 in zip(pair, gates, expanded):
            _, d3 = gate(pre3 + wide(b3.at[1], cols) + x1[slot].astype(F32) * 0.5)
            g = cot[row] * inside(mask, row, cot.shape[1]) * d3
            gsum[slot] = g
            put_mid2(row, slot, mm(we_back[1], g).astype(BF16) * d2)
            terms.append((y2, g))
            if edges:
                second[slot] = y2
        if not edges:
            dexp[...] += mm_nt_sum(terms)

    conv_rows(edges, rows, first1, halos, kf.at[1], kf2.at[1], False, work)


def turn_inner(mask, first1, x1, cot, kf, kf2, b2, we, b3, we_back, gsum, gmid2, dexp):
    start_sums(None, [dexp])

    def put_mid2(row, slot, value):
        gmid2[slot] = value

    turn_rows(False, mask, first1, None, x1, cot, kf, kf2, b2, we, b3, we_back, gsum, dexp, put_mid2)


def turn_edge(mask, first1, above, below, x1, cot, kf, kf2, b2, we, b3, we_back, gmid2_inner,
              gsum, gmid2, second, top, bottom):

    def put_mid2(row, slot, value):
        (bottom if slot else top)[...] = value

    turn_rows(True, mask, first1, (above, below), x1, cot, kf, kf2, b2, we, b3, we_back, gsum, None, put_mid2, second)
    gather_rows(gmid2, gmid2_inner, top, bottom)


def backward_rows(edges, mask, gmid2, g_halos, first1, slope1, x1, gsum1, slope3, slope2,
                  kb, kb2, wr_back, we_back, gsum0, dred, dspat, put_mid2):
    rows, cols = gmid2.shape[0], gmid2.shape[-1]

    def work(pair):
        firsts = [back.astype(BF16) * slope1[slot] for _, slot, back in pair]
        dred[...] += mm_nt_sum([(g1, x1[slot]) for g1, (_, slot, _) in zip(firsts, pair)])
        if not edges:
            dspat[...] += tap_terms(first1, gmid2, [row for row, _, _ in pair])
        ups = both(wr_back[1], firsts)
        for (row, slot, _), g1, up in zip(pair, firsts, ups):
            g = (up + gsum1[slot].astype(F32)).astype(BF16) * slope3[slot] * inside(mask, row, slope3.shape[1])
            gsum0[slot] = g
            put_mid2(row, slot, mm(we_back[0], g).astype(BF16) * slope2[slot])

    conv_rows(edges, rows, gmid2, g_halos, kb.at[1], kb2.at[1], True, work)


def backward_inner(mask, gmid2, first1, f_above, f_below, second_edge, gsum_edge, dexp_turn, slope1, x1, gsum1, slope3, slope2, kb, kb2, wr_back, we_back,
                   gsum0, gmid2_0, dred, dspat, dexp):
    start_sums(None, [dred])
    dspat[...] = edge_tap_terms(first1, (f_above, f_below), gmid2)
    dexp[...] = dexp_turn[...] + mm_nt_sum([(second_edge[n], gsum_edge[n]) for n in range(2)])

    def put_mid2(row, slot, value):
        gmid2_0[slot] = value

    backward_rows(False, mask, gmid2, None, first1, slope1, x1, gsum1, slope3, slope2,
                  kb, kb2, wr_back, we_back, gsum0, dred, dspat, put_mid2)


def backward_edge(mask, gmid2, above, below, slope1, x1, gsum1, slope3, slope2,
                  kb, kb2, wr_back, we_back, gmid2_inner, dred_inner,
                  gsum0, gmid2_0, dred, top, bottom):
    start_sums([dred_inner], [dred])

    def put_mid2(row, slot, value):
        (bottom if slot else top)[...] = value

    backward_rows(True, mask, gmid2, (above, below), None, slope1, x1, gsum1, slope3,
                  slope2, kb, kb2, wr_back, we_back, gsum0, dred, None, put_mid2)
    gather_rows(gmid2_0, gmid2_inner, top, bottom)


def last_rows(edges, gmid2, g_halos, first0, slope1, x, kb, kb2, gmid1, dred, dspat):
    def work(pair):
        firsts = []
        for row, slot, back in pair:
            g1 = back.astype(BF16) * slope1[slot]
            gmid1[slot] = g1
            firsts.append((g1, x[row]))
        dred[...] += mm_nt_sum(firsts)
        if not edges:
            dspat[...] += tap_terms(first0, gmid2, [row for row, _, _ in pair])

    conv_rows(edges, gmid2.shape[0], gmid2, g_halos, kb.at[0], kb2.at[0], True, work, False)


def last_inner(gmid2, first0, f_above, f_below, slope1, x, second_inner, second_edge, gsum_inner, gsum_edge, kb, kb2,
               gmid1, dred, dspat, dexp):
    start_sums(None, [dred])
    dspat[...] = edge_tap_terms(first0, (f_above, f_below), gmid2)
    dexp[...] = mm_nt(second_edge[0], gsum_edge[0]) + mm_nt(second_edge[1], gsum_edge[1])

    @pl.loop(0, second_inner.shape[0] // 2)
    def _(i):
        dexp[...] += mm_nt_sum([(second_inner[2 * i], gsum_inner[2 * i]), (second_inner[2 * i + 1], gsum_inner[2 * i + 1])])

    last_rows(False, gmid2, None, first0, slope1, x, kb, kb2, gmid1, dred, dspat)


def tap_places(mid):
    places = []
    for n in range(9):
        a, b = divmod(n, 3)
        if n < 8:
            base, at = (2 + n // 4) * mid, n % 4
            places.append((slice(a * mid, (a + 1) * mid), slice(b * mid, (b + 1) * mid),
                           slice(base, base + mid), slice(at * mid, (at + 1) * mid)))
        else:
            part = mid // 4
            for q in range(4):
                places.append((slice(a * mid + q * part, a * mid + (q + 1) * part), slice(b * mid, (b + 1) * mid),
                               slice(4 * mid, 4 * mid + part), slice(q * mid, (q + 1) * mid)))
    return places


def last_edge(gmid2, above, below, slope1, x, kb, kb2, dred_inner, dspat,
              dred1, dexp0, dexp1, dspat1, gmid1, keep, send, dred):
    start_sums([dred_inner], [dred])
    last_rows(True, gmid2, (above, below), None, slope1, x, kb, kb2, gmid1, dred, None)
    core = lax.axis_index("batch") % 2

    def pack(out, reduce_term, expand_term, spatial_term):
        mid = reduce_term.shape[0]
        out[:mid] = reduce_term[...].astype(BF16)
        out[mid : 2 * mid] = expand_term[...].astype(BF16)
        for rows_in, cols_in, rows_out, cols_out in tap_places(mid):
            out[rows_out, cols_out] = spatial_term[rows_in, cols_in].astype(BF16)

    for own in range(2):
        @pl.when(core == own)
        def _():
            blocks = ((dred, dexp0, dspat), (dred1, dexp1, dspat1))
            pack(keep, *blocks[own])
            pack(send, *blocks[1 - own])


def grad_rows(gmid1_inner, gmid1_edge, gsum_inner, gsum_edge, wr_back, out, held, sems):
    rows = held.shape[0]

    def work(at, slots, gmid1, gsum):
        for row, slot, acc in zip(at, slots, both(wr_back[0], [gmid1[slot] for slot in slots])):
            held[row] = (acc + gsum[slot].astype(F32) * 0.25).astype(BF16)
            pltpu.make_async_copy(held.at[row], out.at[row], sems.at[row]).start()

    @pl.loop(0, (rows - 2) // 2, unroll=True)
    def _(i):
        work((2 * i + 1, 2 * i + 2), (2 * i, 2 * i + 1), gmid1_inner, gsum_inner)

    work((0, rows - 1), (0, 1), gmid1_edge, gsum_edge)
    for r in range(rows):
        pltpu.make_async_copy(held.at[r], out.at[r], sems.at[r]).wait()


def finish(factor, mine, other, scale_out, g_reduce, g_spatial, g_expand):
    mid = g_reduce.shape[1]
    core = lax.axis_index("batch") % 2
    for terms, k in ((mine, core), (other, 1 - core)):
        g_reduce[k] = terms[:mid].astype(F32) * factor
        scale = jnp.where(k == 0, scale_out[0:1, :] * (factor * 0.25), scale_out[1:2, :] * (factor * 0.5))
        g_expand[k] = terms[mid : 2 * mid].astype(F32) * scale
        for rows_in, cols_in, rows_out, cols_out in tap_places(mid):
            a, b = rows_in.start // mid, cols_in.start // mid
            part = terms[rows_out, cols_out].astype(F32) * factor
            g_spatial[k, a, b, rows_in.start - a * mid : rows_in.stop - a * mid] = part


def lanes(vector, count):
    return jnp.broadcast_to(vector, (count, vector.shape[-1])).T


def twin(out, k, value):
    tall, across = value.shape
    out[k, :tall, :across] = value
    out[k, tall:, across:] = value


def start(limits, images, red_h, spa_h, exp_h, sm_h, sh_h, so_h, sho_h,
          mask, wr, b1, red, spa, exp, scale_mid, shift_mid, scale_out, shift_out, slope1, top, bottom, x, sems):
    rows, cols = images.shape[0], x.shape[-1]
    copies = [pltpu.make_async_copy(s, d, sems.at[n]) for n, (s, d) in enumerate(
        ((sm_h, scale_mid), (sh_h, shift_mid), (red_h, red), (images.at[0], x.at[0]), (images.at[rows - 1], x.at[1]),
         (spa_h, spa), (exp_h, exp), (so_h, scale_out), (sho_h, shift_out)))]
    for copy in copies:
        copy.start()
    for copy in copies[:3]:
        copy.wait()
    for row in range(rows):
        mask[row] = jnp.broadcast_to(row_mask(limits, row, cols), mask.shape[1:])
    wr[...] = (red[0].astype(F32) * (0.5 * lanes(scale_mid[0, 0:1, :], red.shape[-1]))).astype(BF16)
    b1[...] = 0.5 * lanes(shift_mid[0, 0:1, :], b1.shape[-1])
    for slot, (row, edge) in enumerate(((0, top), (rows - 1, bottom))):
        copies[3 + slot].wait()
        edge[...], slope1[slot] = reduce_part(x[slot], wr, b1, inside(mask, row, edge.shape[0]))
    for copy in copies[5:]:
        copy.wait()


def prepare(red, spa, exp, scale_mid, shift_mid, scale_out, shift_out,
            wr, kf, kf2, we, we_back, kb, kb2, wr_back, b1, b2, b3):
    mid = red.shape[1]
    for out in (kf2, kb2, we, wr_back):
        out[...] = jnp.zeros_like(out)
    for k in range(2):
        twice = 2.0 ** (2 - k)
        s1, s2 = scale_mid[k, 0:1, :], scale_mid[k, 1:2, :]
        so = scale_out[k : k + 1, :]
        r, e = red[k].astype(F32), exp[k].astype(F32)
        chans = r.shape[-1]
        if k == 1:
            wr[...] = (r * (0.5 * lanes(s1, chans))).astype(BF16)
            b1[...] = 0.5 * lanes(shift_mid[k, 0:1, :], b1.shape[-1])
        twin(wr_back, k, (r * (1.0 if k == 0 else twice)).T.astype(BF16))
        twin(we, k, (e * (0.5 * so)).T.astype(BF16))
        we_back[k] = (e * (so * (0.5 / twice)) * lanes(s2, chans)).astype(BF16)
        half = 0.5 * lanes(s1, mid)
        for a in range(3):
            for b in range(3):
                part = spa[k, a, b].astype(F32)
                ahead = (part * (0.5 * s2)).T.astype(BF16)
                back = (part * half).astype(BF16)
                for out, out2, value, at in ((kf, kf2, ahead, a), (kb, kb2, back, 2 - a)):
                    out[k, b * mid : (b + 1) * mid, at * mid : (at + 1) * mid] = value
                    for j in range(2):
                        out2[k, (3 * j + b) * mid : (3 * j + b + 1) * mid, (at + j) * mid : (at + j + 1) * mid] = value
        b2[k] = 0.5 * lanes(shift_mid[k, 1:2, :], b2.shape[-1])
        b3[k] = 0.5 * lanes(shift_out[k : k + 1, :], b3.shape[-1])


def call(kernel, outs, args, name, specs=None, out_specs=None, scratch=(), limit=VMEM_LIMIT):
    return pl.pallas_call(
        kernel,
        in_specs=specs or [VMEM] * len(args),
        out_specs=out_specs or [VMEM] * len(outs),
        out_shape=[jax.ShapeDtypeStruct(s, d) for s, d in outs],
        scratch_shapes=list(scratch),
        compiler_params=pltpu.CompilerParams(vmem_limit_bytes=limit),
        name=name,
    )(*args)


def exchange(top, bottom):
    count = lax.axis_size("space")
    below = lax.ppermute(top, "space", [((i + 1) % count, i) for i in range(count)])
    above = lax.ppermute(bottom, "space", [(i, (i + 1) % count) for i in range(count)])
    return above, below


def swaps():
    def flat(z, x, core, y):
        return ((z % 2 * 4 + x) * 2 + core) * 8 + y * 2 + z // 2

    places = [(z, x, core, y) for z in range(4) for x in range(4) for core in range(2) for y in range(4)]
    orders = ((1, 3, 0), (3, 0, 1))
    steps = []
    for turn in range(3):
        steps.append([[(flat(*at), flat(*(c ^ mirror if n == orders[at[2]][turn] else c for n, c in enumerate(at))))
                       for at in places] for mirror in (1, 3, 2)])
    return steps


def all_sum(keep, send, beside):
    cores = [(i, i ^ 1) for i in range(lax.axis_size("batch"))]
    value = keep.astype(F32) + lax.ppermute(send, "batch", cores).astype(F32)
    for step, ring in enumerate(swaps()):
        if step == BESIDE:
            value, beside = lax.optimization_barrier((value, beside))
        rounded = value.astype(BF16)
        for got in [lax.ppermute(rounded, ("batch", "space"), pairs) for pairs in ring]:
            value = value + got.astype(F32)
    mine = value.astype(BF16)
    return mine, lax.ppermute(mine, "batch", cores), beside


def body(images, heights, widths, conv_reduce, conv_spatial, conv_expand, scale_mid, shift_mid,
         scale_out, shift_out, cotangent):
    _, rows, chans, cols = images.shape
    mid = conv_reduce.shape[-1]
    cot = cotangent[0]
    wide_w, tall_w = ((mid, chans), BF16), ((2 * chans, 2 * mid), BF16)
    single, double = ((3 * mid, 3 * mid), BF16), ((6 * mid, 4 * mid), BF16)
    bias = ((mid, 128), F32)
    made = [single, double, tall_w, wide_w, single, double, tall_w]
    params = [conv_reduce.swapaxes(1, 2), conv_spatial, conv_expand, scale_mid, shift_mid, scale_out, shift_out]

    def small(count):
        return (count, mid, cols), BF16

    def large(count):
        return (count, chans, cols), BF16

    inner, edge = rows - 2, 2
    row = ((mid, cols), BF16)
    acc_c = ((mid, chans), F32)
    acc_s = ((3 * mid, 3 * mid), F32)

    ids = lax.axis_index("space") * rows + lax.broadcasted_iota(jnp.int32, (rows, 128), 0)
    limits = jnp.where(ids < heights, widths, 0)
    strip = pltpu.with_memory_space_constraint(images[0], pltpu.HBM)
    mask, wr_0, b1_0, *held, slope1_0e, top, bottom = call(
        start, [((rows, 16, cols), BF16), wide_w, bias] + [(p.shape, p.dtype) for p in params] + [small(edge), row, row],
        [limits, strip] + [pltpu.with_memory_space_constraint(p, pltpu.HBM) for p in params],
        "start", [VMEM] + [HBM] * 8, scratch=[pltpu.VMEM(*large(edge)), pltpu.SemaphoreType.DMA((2 + len(params),))])
    f0a, f0b = exchange(top, bottom)
    hw = [mask]
    first0, slope1_0i, second0i, slope2_0i, slope3_0i, x1i, slope1_1i, first1i, *weights = call(
        forward_inner, [small(rows)] + [small(inner)] * 3 + [large(inner)] * 2 + [small(inner)] * 2
        + [wide_w] + [((2,) + s, d) for s, d in made] + [bias] + [((2,) + s, d) for s, d in (bias, ((chans, 128), F32))],
        hw + [images[0], top, bottom, wr_0, b1_0] + held, "forward_inner")
    wr, kf, kf2, we, we_back, kb, kb2, wr_back, b1, b2, b3 = weights
    second0e, slope2_0e, slope3_0e, x1e, slope1_1e, first1, top, bottom = call(
        forward_edge, [small(edge)] * 2 + [large(edge)] * 2 + [small(edge), small(rows), row, row],
        hw + [images[0], first0, f0a, f0b, first1i, kf, kf2, b2, we, b3, wr, b1], "forward_edge")
    f1a, f1b = exchange(top, bottom)
    turn = [kf, kf2, b2, we, b3, we_back]
    gsum1i, gmid2_1i, dexp1 = call(
        turn_inner, [large(inner), small(inner), acc_c], hw + [first1, x1i, cot] + turn, "turn_inner")
    gsum1e, gmid2_1, second1e, top, bottom = call(
        turn_edge, [large(edge), small(rows), small(edge), row, row],
        hw + [first1, f1a, f1b, x1e, cot] + turn + [gmid2_1i], "turn_edge")
    g1a, g1b = exchange(top, bottom)
    back = [kb, kb2, wr_back, we_back]
    gsum0i, gmid2_0i, dred1, dspat1, dexp1 = call(
        backward_inner, [large(inner), small(inner), acc_c, acc_s, acc_c],
        hw + [gmid2_1, first1, f1a, f1b, second1e, gsum1e, dexp1, slope1_1i, x1i, gsum1i, slope3_0i, slope2_0i] + back, "backward_inner")
    gsum0e, gmid2_0, dred1, top, bottom = call(
        backward_edge, [large(edge), small(rows), acc_c, row, row],
        hw + [gmid2_1, g1a, g1b, slope1_1e, x1e, gsum1e, slope3_0e, slope2_0e] + back + [gmid2_0i, dred1], "backward_edge")
    g0a, g0b = exchange(top, bottom)
    gmid1_0i, dred0, dspat0, dexp0 = call(
        last_inner, [small(inner), acc_c, acc_s, acc_c],
        [gmid2_0, first0, f0a, f0b, slope1_0i, images[0], second0i, second0e, gsum0i, gsum0e, kb, kb2], "last_inner")
    gmid1_0e, keep, send = call(
        last_edge, [small(edge), ((4 * mid + mid // 4, chans), BF16), ((4 * mid + mid // 4, chans), BF16)],
        [gmid2_0, g0a, g0b, slope1_0e, images[0], kb, kb2, dred0, dspat0, dred1, dexp0, dexp1, dspat1],
        "last_edge", scratch=[pltpu.VMEM(*acc_c)])
    (grad,) = call(
        grad_rows, [large(rows)], [gmid1_0i, gmid1_0e, gsum0i, gsum0e, wr_back], "grad_images", out_specs=[HBM],
        scratch=[pltpu.VMEM(*large(rows)), pltpu.SemaphoreType.DMA((rows,))])
    mine, other, grad = all_sum(keep, send, grad)
    factor = 1.0 / math.sqrt(lax.axis_size("batch") * rows * lax.axis_size("space") * cols)
    g_reduce, g_spatial, g_expand = call(
        functools.partial(finish, factor),
        [((2, mid, chans), F32), (conv_spatial.shape, F32), ((2, mid, chans), F32)], [mine, other, scale_out], "finish")
    return grad[None], g_reduce.swapaxes(1, 2), g_spatial, g_expand


def solution(mesh):
    strips = P("batch", "space", None, None)
    placed = (strips, P("batch"), P("batch")) + (P(),) * 7 + (strips,)
    return jax.shard_map(
        body, mesh=mesh, in_specs=placed, out_specs=(strips, P(), P(), P()), check_vma=False)
```
